128 devices in a mesh: dp: 16 (over x, y_lo, core), expert: 8 (over y_hi, z).
Axes of the slice: x: 4, y: 4 (y_hi: 2, y_lo: 2; y = y_hi * 2 + y_lo), z: 4, core: 2. Of those that a mesh axis runs over, the one named last changes fastest.
Arguments:
- tokens: bfloat16 [256, 256, 1280], P(('dp', 'expert')), may hold values from -5 to 5, as said below
- slot_param: bfloat16 [32, 1280], replicated, may hold values from -0.1 to 0.1
- inner_weight: bfloat16 [32, 5120, 1280], P('expert', 'dp'), may hold values from -0.15625 to 0.15625
- outer_weight: bfloat16 [32, 5120, 1280], P('expert', 'dp'), may hold values from -0.078125 to 0.078125
- output_grad: bfloat16 [256, 256, 1280], P(('dp', 'expert')), may hold values from -6 to 6
Outputs:
- grad_tokens: bfloat16 [256, 256, 1280], P(('dp', 'expert'))
- grad_param: float32 [32, 1280], replicated
- grad_inner: bfloat16 [32, 5120, 1280], P('expert', 'dp')
- grad_outer: bfloat16 [32, 5120, 1280], P('expert', 'dp')
The draws below stay inside these ranges and needn't reach their ends.
Inputs may be any that keep to these rules, and one draw needn't show every extreme that they name: `tokens`: saved patch rows of order one.
All inputs are finite; a program needn't handle non-finite values.
Results may differ from the reference program's by a relative error of at most 0.03.
Values may be sent and summed in bfloat16 or wider, within the bound.
A program may use at most 128 MiB of HBM per device.

```python
import jax
import jax.numpy as jnp
from jax import lax

D = 1280
FF = 5120
PATCHES = 256
EXPERTS = 32
IMAGES = 256
N_DP = 16


def shared_signs(key):
    return (jax.random.randint(key, (EXPERTS, D), 0, 2) * 2 - 1).astype(jnp.float32)


def draw_slot_param(key, part):
    sign_table = shared_signs(key)
    key = jax.random.fold_in(key, 11)
    key_size = jax.random.fold_in(key, 0)
    magnitude = jax.random.uniform(key_size, (EXPERTS, D), minval=0.06, maxval=0.0995)
    values = sign_table * magnitude
    return values.astype(jnp.bfloat16)


def draw_tokens(key, part):
    key = jax.random.fold_in(key, 5)
    key_rows = jax.random.fold_in(key, 0)
    patch_rows = jnp.clip(jax.random.normal(key_rows, (IMAGES, PATCHES, D)), -5.0, 5.0)
    return patch_rows.astype(jnp.bfloat16)


def level_of(rng, dims, cuts, smallest, largest):
    def one(position, shards_of):
        steps = jax.random.uniform(jax.random.fold_in(jax.random.fold_in(rng, 6), position), (shards_of,), jnp.float32, smallest / len(cuts), largest / len(cuts))
        return jnp.repeat(jnp.exp(steps), dims[position] // shards_of).reshape((-1,) + (1,) * (len(dims) - position - 1))

    loudness = one(*cuts[0])
    for cut in cuts[1:]:
        loudness = loudness * one(*cut)
    return loudness


def gaussian(own_key, shape, width, bound, cuts=(), dtype=jnp.bfloat16):
    array = jax.random.normal(own_key, shape, jnp.float32) * width
    if len(cuts) > 0:
        array = level_of(own_key, shape, cuts, -0.22, 0.18) * array
    return jnp.clip(array, min=-bound, max=bound).astype(dtype)


def setup_inputs(seed: int = 0) -> dict:
    key_list = jax.random.split(jax.random.key(seed), 6)
    return {
        "tokens": draw_tokens(jax.random.fold_in(key_list[5], 71), 0),
        "slot_param": draw_slot_param(jax.random.fold_in(key_list[5], 71), 0),
        "inner_weight": gaussian(key_list[2], (EXPERTS, FF, D), D ** -0.5, 0.15625, ((0, 8), (1, 16))),
        "outer_weight": gaussian(key_list[3], (EXPERTS, FF, D), FF ** -0.5, 0.078125, ((0, 8), (1, 16))),
        "output_grad": gaussian(key_list[4], (IMAGES, PATCHES, D), 1.0, 6.0, ((0, 128),)),
    }


def gelu_slope(values):
    return 0.5 * (1.0 + jax.scipy.special.erf(values * 0.7071067811865476)) + values * jnp.exp(-0.5 * values * values) * 0.3989422804014327


def route(image_rows, slot_param):
    logits = jnp.dot(slot_param, image_rows.T, preferred_element_type=jnp.float32)
    dispatch = jax.nn.softmax(logits, axis=1)
    combine = jax.nn.softmax(logits, axis=0)
    return dispatch, combine


def reference(tokens, slot_param, inner_weight, outer_weight, output_grad):
    def forward_slots(operands):
        image_rows, image_grad = operands
        dispatch, combine = route(image_rows, slot_param)
        slot_inputs = jnp.dot(dispatch.astype(jnp.bfloat16), image_rows, preferred_element_type=jnp.float32).astype(jnp.bfloat16)
        slot_grads = jnp.dot(combine.astype(jnp.bfloat16), image_grad, preferred_element_type=jnp.float32).astype(jnp.bfloat16)
        return slot_inputs, slot_grads

    slot_inputs, slot_grads = lax.map(forward_slots, (tokens, output_grad))
    block_size = FF // N_DP

    def expert_step(operands):
        rows_in, rows_grad, weight_in, weight_out = operands
        hidden = jnp.dot(rows_in, weight_in.T, preferred_element_type=jnp.float32)
        active = jax.nn.gelu(hidden, approximate=False).astype(jnp.bfloat16)
        partial_value = jnp.einsum('ipf,pfd->ipd', active.reshape(-1, N_DP, block_size).astype(jnp.float32), weight_out.reshape(N_DP, block_size, -1).astype(jnp.float32))
        slot_out = jnp.sum(partial_value.astype(jnp.bfloat16).astype(jnp.float32), axis=1).astype(jnp.bfloat16)
        active_grad = jnp.dot(rows_grad, weight_out.T, preferred_element_type=jnp.float32)
        scaled = (active_grad * gelu_slope(hidden)).astype(jnp.bfloat16)
        grad_out = jnp.dot(active.T, rows_grad, preferred_element_type=jnp.float32).astype(jnp.bfloat16)
        grad_in = jnp.dot(scaled.T, rows_in, preferred_element_type=jnp.float32).astype(jnp.bfloat16)
        back_terms = jnp.einsum('ipf,pfd->ipd', scaled.reshape(-1, N_DP, block_size).astype(jnp.float32), weight_in.reshape(N_DP, block_size, -1).astype(jnp.float32))
        slot_back = jnp.sum(back_terms.astype(jnp.bfloat16).astype(jnp.float32), axis=1).astype(jnp.bfloat16)
        return slot_out, slot_back, grad_in, grad_out

    slot_out, slot_back, grad_inner, grad_outer = lax.map(expert_step, (jnp.transpose(slot_inputs, (1, 0, 2)), jnp.transpose(slot_grads, (1, 0, 2)), inner_weight, outer_weight))
    slot_out = jnp.transpose(slot_out, (1, 0, 2))
    slot_back = jnp.transpose(slot_back, (1, 0, 2))

    def backward_image(operands):
        image_rows, image_grad, outs_one, backs_one = operands
        dispatch, combine = route(image_rows, slot_param)
        combine_grad = jnp.dot(outs_one, image_grad.T, preferred_element_type=jnp.float32)
        combine_term = combine * (combine_grad - jnp.sum(combine * combine_grad, axis=0, keepdims=True))
        dispatch_grad = jnp.dot(backs_one, image_rows.T, preferred_element_type=jnp.float32)
        dispatch_term = dispatch * (dispatch_grad - jnp.sum(dispatch * dispatch_grad, axis=1, keepdims=True))
        logit_grad = (combine_term + dispatch_term).astype(jnp.bfloat16)
        grad_rows = (jnp.dot(dispatch.astype(jnp.bfloat16).T, backs_one, preferred_element_type=jnp.float32) + jnp.dot(logit_grad.T, slot_param, preferred_element_type=jnp.float32)).astype(jnp.bfloat16)
        param_term = jnp.dot(logit_grad, image_rows, preferred_element_type=jnp.float32)
        return grad_rows, param_term

    grad_tokens, param_terms = lax.map(backward_image, (tokens, output_grad, slot_out, slot_back))
    grad_param = jnp.sum(param_terms, axis=0)
    return grad_tokens, grad_param, grad_inner, grad_outer
```

```python
import functools

import jax
import jax.numpy as jnp
from jax import lax
from jax.experimental import pallas as pl
from jax.experimental.pallas import tpu as pltpu
from jax.sharding import PartitionSpec as P

MESH = pl.DeviceIdType.MESH
F32 = jnp.float32
BF16 = jnp.bfloat16
NX, NY, NC = 4, 2, 2
GROUPS = 8
LOCAL = 4
IMGS = 2
SLOTS = GROUPS * LOCAL
ROWS = 16
BLOCKS = NC * NY * NX
D = 1280
PATCHES = 256
HIDDEN = 320
TILE = 256
STEPS = D // TILE


def dot(a, b, ca=1, cb=0):
    return lax.dot_general(a, b, (((ca,), (cb,)), ((), ())), preferred_element_type=F32)


def permutation(source_of):
    size = 2 * IMGS * SLOTS
    row = lax.broadcasted_iota(jnp.int32, (size, size), 0)
    column = lax.broadcasted_iota(jnp.int32, (size, size), 1)
    return jnp.where(column == source_of(row), 1.0, 0.0).astype(BF16)


def slots_to_messages(r):
    group, array, expert, image = r // 16, (r // 8) % 2, (r // 2) % 4, r % 2
    return array * 64 + image * 32 + group * 4 + expert


def messages_to_slots(r):
    array, image, group, expert = r // 64, (r // 32) % 2, (r // 4) % 8, r % 4
    return group * 16 + array * 8 + expert * 2 + image


def messages_to_blocks(r):
    array, expert, group, image = r // 64, (r // 16) % 4, (r // 2) % 8, r % 2
    return group * 16 + array * 8 + expert * 2 + image


def blocks_to_messages(r):
    group, array, expert, image = r // 16, (r // 8) % 2, (r // 2) % 4, r % 2
    return array * 64 + expert * 16 + group * 2 + image


def kernel(
    tokens, slot_param, inner, outer, cotangent,
    grad_tokens, grad_param, grad_inner, grad_outer,
    T, G, SP, WI, WO, DI, CO, X, MSG, MSG_IN, BACK, BACK_IN, FIN, SUMS,
    R, PART, SIB, RY0, RX0, RY1, RX1,
    PP, AR1, S1, AR2, S2, AR3, AR4, S4, GP,
    in_sem, a2a_s, a2a_r, back_s, back_r, ag_s, ag_r, rs_s, rs_r, ar_s, ar_r,
):
    dp, ex = lax.axis_index("dp"), lax.axis_index("expert")
    x, y, c = dp // 4, (dp // 2) % 2, dp % 2

    def at_dp(px, py, pc):
        return (px * 4 + py * 2 + pc, ex)

    def right(k):
        return (x + k) % NX

    def left(k):
        return (x + NX - k) % NX

    def to_x(k):
        return at_dp(right(k), y, c)

    to_y = at_dp(x, 1 - y, c)
    to_core = at_dp(x, y, 1 - c)

    def ex_to(k):
        return (ex + k) % GROUPS

    def ex_from(k):
        return (ex + GROUPS - k) % GROUPS

    def remote(src, dst, send, recv, device):
        return pltpu.make_async_remote_copy(
            src_ref=src, dst_ref=dst, send_sem=send, recv_sem=recv, device_id=device, device_id_type=MESH
        )

    barrier = pltpu.get_barrier_semaphore()
    for k in range(1, GROUPS):
        pl.semaphore_signal(barrier, inc=1, device_id=(dp, ex_to(k)), device_id_type=MESH)
    for k in range(1, NX):
        pl.semaphore_signal(barrier, inc=1, device_id=to_x(k), device_id_type=MESH)
    pl.semaphore_signal(barrier, inc=1, device_id=to_y, device_id_type=MESH)
    pl.semaphore_signal(barrier, inc=1, device_id=to_core, device_id_type=MESH)

    loads = [
        pltpu.make_async_copy(slot_param, SP, in_sem.at[0]),
        pltpu.make_async_copy(tokens, T, in_sem.at[1]),
        pltpu.make_async_copy(cotangent, G, in_sem.at[2]),
        pltpu.make_async_copy(inner, WI, in_sem.at[3]),
        pltpu.make_async_copy(outer, WO, in_sem.at[4]),
    ]
    for load in loads:
        load.start()
    for load in loads[:3]:
        load.wait()

    for i in range(IMGS):
        logits = dot(SP[...], T[i], 1, 1)
        ed = jnp.exp(logits - jnp.max(logits, axis=1, keepdims=True))
        dispatch = ed / jnp.sum(ed, axis=1, keepdims=True)
        ec = jnp.exp(logits - jnp.max(logits, axis=0, keepdims=True))
        combine = ec / jnp.sum(ec, axis=0, keepdims=True)
        DI[i] = dispatch
        CO[i] = combine
        X[i] = dot(dispatch.astype(BF16), T[i]).astype(BF16)
        X[IMGS + i] = dot(combine.astype(BF16), G[i]).astype(BF16)
    MSG[...] = (
        dot(permutation(slots_to_messages), X[...].reshape(2 * IMGS * SLOTS, D))
        .astype(BF16).reshape(GROUPS, ROWS, D)
    )

    pl.semaphore_wait(barrier, GROUPS - 1 + NX - 1 + 2)

    def a2a(k):
        return remote(MSG.at[ex_to(k)], MSG_IN.at[ex], a2a_s.at[k], a2a_r.at[k], (dp, ex_to(k)))

    for k in range(1, GROUPS):
        a2a(k).start()
    MSG_IN[ex] = MSG[ex]
    for k in range(1, GROUPS):
        a2a(k).wait_recv()
    blocks = (
        dot(permutation(messages_to_blocks), MSG_IN[...].reshape(2 * IMGS * SLOTS, D))
        .astype(BF16).reshape(2, LOCAL, ROWS, D)
    )
    for a in range(2):
        for e in range(LOCAL):
            R[a, e, c, y, x] = blocks[a, e]

    def block_copy(a, e, py, px, sem, device):
        ref = R.at[a, e, c, py, px]
        return remote(ref, ref, ag_s.at[a, e, sem], ag_r.at[a, e, sem], device)

    def gather_first(e, act):
        for k in range(1, NX):
            act(block_copy(0, e, y, x, k - 1, to_x(k)))
        act(block_copy(1, e, y, x, 3, to_y))
        for k in range(1, NX):
            act(block_copy(1, e, y, x, k - 1, to_x(k)))
        act(block_copy(0, e, y, x, 3, to_y))

    def gather_second_x(e, act, k):
        act(block_copy(1, e, 1 - y, x, 3 + k, to_x(k)))

    def gather_second_y(e, act, k):
        act(block_copy(0, e, y, left(k), 3 + k, to_y))

    def gather_third(e, act):
        for a in range(2):
            ref = R.at[a, e, c]
            act(remote(ref, ref, ag_s.at[a, e, 7], ag_r.at[a, e, 7], to_core))

    def start(copy):
        copy.start()

    def wait_send(copy):
        copy.wait_send()

    def wait_recv(a, e, sem):
        block_copy(a, e, y, x, sem, to_y).wait_recv()

    def second(e):
        wait_recv(1, e, 3)
        for k in range(1, NX):
            gather_second_x(e, start, k)
        for k in (1, 3, 2):
            wait_recv(0, e, k - 1)
            gather_second_y(e, start, k)

    def third(e):
        for sem in (0, 1, 2, 4, 5, 6):
            wait_recv(1, e, sem)
        for sem in (3, 4, 5, 6):
            wait_recv(0, e, sem)
        gather_third(e, start)

    def expert(e):
        for a in range(2):
            ref = R.at[a, e, c]
            remote(ref, ref, ag_s.at[a, e, 7], ag_r.at[a, e, 7], to_core).wait_recv()
        rows_in = R[0, e].reshape(BLOCKS * ROWS, D)
        rows_grad = R[1, e].reshape(BLOCKS * ROWS, D)
        hidden = dot(WI[e], rows_in, 1, 1)
        slope = dot(WO[e], rows_grad, 1, 1)
        phi = 0.5 * (1.0 + lax.erf(hidden * 0.7071067811865476))
        active = (hidden * phi).astype(BF16)
        scaled = (slope * (phi + hidden * jnp.exp(-0.5 * hidden * hidden) * 0.3989422804014327)).astype(BF16)
        active_t = active.T
        scaled_t = scaled.T
        for n in range(STEPS):
            cols = slice(n * TILE, (n + 1) * TILE)
            PART[0, e, :, :, :, :, cols] = (
                dot(active_t, WO[e, :, cols]).astype(BF16).reshape(NC, NY, NX, ROWS, TILE)
            )
            PART[1, e, :, :, :, :, cols] = (
                dot(scaled_t, WI[e, :, cols]).astype(BF16).reshape(NC, NY, NX, ROWS, TILE)
            )
        sums_core(e, start)
        for n in range(STEPS):
            cols = slice(n * TILE, (n + 1) * TILE)
            grad_outer[e, :, cols] = dot(active, rows_grad[:, cols]).astype(BF16)
            grad_inner[e, :, cols] = dot(scaled, rows_in[:, cols]).astype(BF16)

    def sum_copy(a, e, src, dst, sem, device):
        return remote(src, dst, rs_s.at[a, e, sem], rs_r.at[a, e, sem], device)

    def sums_core(e, act):
        for a in range(2):
            act(sum_copy(a, e, PART.at[a, e, 1 - c], SIB.at[a, e], 0, to_core))

    def sums_y0(e):
        return sum_copy(0, e, PART.at[0, e, c, 1 - y], RY0.at[e], 4, to_y)

    def sums_x0(e, k):
        return sum_copy(0, e, PART.at[0, e, c, y, right(k)], RX0.at[e, k - 1], k, to_x(k))

    def sums_x1(e, k):
        return sum_copy(1, e, PART.at[1, e, c, :, right(k)], RX1.at[e, k - 1], k, to_x(k))

    def sums_y1(e):
        return sum_copy(1, e, PART.at[1, e, c, 1 - y, x], RY1.at[e], 4, to_y)

    def add_core(e):
        for a in range(2):
            sum_copy(a, e, PART.at[a, e, 1 - c], SIB.at[a, e], 0, to_core).wait_recv()
        for a in range(2):
            PART[a, e, c] = (PART[a, e, c].astype(F32) + SIB[a, e].astype(F32)).astype(BF16)
            if a == 0:
                sums_y0(e).start()
            else:
                for k in range(1, NX):
                    sums_x1(e, k).start()

    def add_second(e):
        sums_y0(e).wait_recv()
        PART[0, e, c, y] = (PART[0, e, c, y].astype(F32) + RY0[e].astype(F32)).astype(BF16)
        for k in range(1, NX):
            sums_x0(e, k).start()
        total = PART[1, e, c, :, x].astype(F32)
        for k in range(1, NX):
            sums_x1(e, k).wait_recv()
            total = total + RX1[e, k - 1].astype(F32)
        PART[1, e, c, :, x] = total.astype(BF16)
        sums_y1(e).start()

    def add_third(e):
        total = PART[0, e, c, y, x].astype(F32)
        for k in range(1, NX):
            sums_x0(e, k).wait_recv()
            total = total + RX0[e, k - 1].astype(F32)
        FIN[0, e] = total.astype(BF16)
        sums_y1(e).wait_recv()
        FIN[1, e] = (PART[1, e, c, y, x].astype(F32) + RY1[e].astype(F32)).astype(BF16)

    def firsts(e, carry):
        gather_first(e, start)
        return carry

    lax.fori_loop(0, LOCAL, firsts, 0)
    for load in loads[3:]:
        load.wait()

    def step(t, carry):
        def stage(lag, work):
            @pl.when(jnp.logical_and(t >= lag, t < LOCAL + lag))
            def _():
                work(t - lag)

        stage(0, second)
        stage(1, third)
        stage(3, add_core)
        stage(4, add_second)
        stage(5, add_third)
        stage(2, expert)
        return carry

    lax.fori_loop(0, LOCAL + 5, step, 0)

    BACK[...] = (
        dot(permutation(blocks_to_messages), FIN[...].reshape(2 * IMGS * SLOTS, D))
        .astype(BF16).reshape(GROUPS, ROWS, D)
    )

    def back(k):
        return remote(BACK.at[ex_to(k)], BACK_IN.at[ex], back_s.at[k], back_r.at[k], (dp, ex_to(k)))

    for k in range(1, GROUPS):
        back(k).start()
    BACK_IN[ex] = BACK[ex]
    for k in range(1, GROUPS):
        back(k).wait_recv()
    SUMS[...] = (
        dot(permutation(messages_to_slots), BACK_IN[...].reshape(2 * IMGS * SLOTS, D))
        .astype(BF16).reshape(2, IMGS, SLOTS, D)
    )

    param = jnp.zeros((SLOTS, D), F32)
    logit_grads = []
    for i in range(IMGS):
        dispatch, combine = DI[i], CO[i]
        combine_grad = dot(SUMS[0, i], G[i], 1, 1)
        dispatch_grad = dot(SUMS[1, i], T[i], 1, 1)
        combine_term = combine * (combine_grad - jnp.sum(combine * combine_grad, axis=0, keepdims=True))
        dispatch_term = dispatch * (dispatch_grad - jnp.sum(dispatch * dispatch_grad, axis=1, keepdims=True))
        logit_grad = (combine_term + dispatch_term).astype(BF16)
        logit_grads.append(logit_grad)
        param = param + dot(logit_grad, T[i])

    for j in range(GROUPS):
        PP[j] = param[8 * (j // 2):8 * (j // 2) + 8, 640 * (j % 2):640 * (j % 2) + 640]

    def ar_scatter(k):
        return remote(PP.at[ex_to(k)], AR1.at[k - 1], ar_s.at[k], ar_r.at[k], (dp, ex_to(k)))

    for k in range(1, GROUPS):
        ar_scatter(k).start()

    for i in range(IMGS):
        both = jnp.concatenate([DI[i].astype(BF16), logit_grads[i]], axis=0)
        rows = jnp.concatenate([SUMS[1, i], SP[...]], axis=0)
        grad_tokens[i] = dot(both.T, rows).astype(BF16)

    total = PP[ex]
    for k in range(1, GROUPS):
        ar_scatter(k).wait_recv()
        total = total + AR1[k - 1]
    S1[...] = total
    ar_core = remote(S1, AR2, ar_s.at[8], ar_r.at[8], to_core)
    ar_core.start()
    ar_core.wait_recv()
    S2[...] = S1[...] + AR2[...]
    ar_y = remote(S2, AR3, ar_s.at[9], ar_r.at[9], to_y)
    ar_y.start()
    ar_y.wait_recv()
    AR4[x] = S2[...] + AR3[...]

    def ar_x(k):
        return remote(AR4.at[x], AR4.at[x], ar_s.at[9 + k], ar_r.at[9 + k], to_x(k))

    for k in range(1, NX):
        ar_x(k).start()
    for k in range(1, NX):
        ar_x(k).wait_recv()
    GP[ex] = (AR4[0] + AR4[1]) + (AR4[2] + AR4[3])

    def ar_gather(k):
        return remote(GP.at[ex], GP.at[ex], ar_s.at[12 + k], ar_r.at[12 + k], (dp, ex_to(k)))

    for k in range(1, GROUPS):
        ar_gather(k).start()

    def drain(e, carry):
        gather_first(e, wait_send)
        for k in range(1, NX):
            gather_second_x(e, wait_send, k)
            gather_second_y(e, wait_send, k)
            sums_x0(e, k).wait_send()
            sums_x1(e, k).wait_send()
        gather_third(e, wait_send)
        sums_core(e, wait_send)
        sums_y0(e).wait_send()
        sums_y1(e).wait_send()
        return carry

    lax.fori_loop(0, LOCAL, drain, 0)
    for k in range(1, GROUPS):
        a2a(k).wait_send()
        back(k).wait_send()
        ar_scatter(k).wait_send()
    ar_core.wait_send()
    ar_y.wait_send()
    for k in range(1, NX):
        ar_x(k).wait_send()
    for k in range(1, GROUPS):
        ar_gather(k).wait_recv()
    for k in range(1, GROUPS):
        ar_gather(k).wait_send()
    for j in range(GROUPS):
        grad_param[8 * (j // 2):8 * (j // 2) + 8, 640 * (j % 2):640 * (j % 2) + 640] = GP[j]


def on_device(tokens, slot_param, inner_weight, outer_weight, output_grad):
    vmem = pl.BlockSpec(memory_space=pltpu.VMEM)
    chunk = (8, D * SLOTS // (8 * GROUPS))
    dma = pltpu.SemaphoreType.DMA
    return pl.pallas_call(
        kernel,
        out_shape=(
            jax.ShapeDtypeStruct(tokens.shape, BF16),
            jax.ShapeDtypeStruct(slot_param.shape, F32),
            jax.ShapeDtypeStruct(inner_weight.shape, BF16),
            jax.ShapeDtypeStruct(outer_weight.shape, BF16),
        ),
        in_specs=[pl.BlockSpec(memory_space=pl.ANY)] * 5,
        out_specs=(vmem,) * 4,
        scratch_shapes=[
            pltpu.VMEM((IMGS, PATCHES, D), BF16),
            pltpu.VMEM((IMGS, PATCHES, D), BF16),
            pltpu.VMEM((SLOTS, D), BF16),
            pltpu.VMEM((LOCAL, HIDDEN, D), BF16),
            pltpu.VMEM((LOCAL, HIDDEN, D), BF16),
            pltpu.VMEM((IMGS, SLOTS, PATCHES), F32),
            pltpu.VMEM((IMGS, SLOTS, PATCHES), F32),
            pltpu.VMEM((2 * IMGS, SLOTS, D), BF16),
            pltpu.VMEM((GROUPS, ROWS, D), BF16),
            pltpu.VMEM((GROUPS, ROWS, D), BF16),
            pltpu.VMEM((GROUPS, ROWS, D), BF16),
            pltpu.VMEM((GROUPS, ROWS, D), BF16),
            pltpu.VMEM((2, LOCAL, ROWS, D), BF16),
            pltpu.VMEM((2, IMGS, SLOTS, D), BF16),
            pltpu.VMEM((2, LOCAL, NC, NY, NX, ROWS, D), BF16),
            pltpu.VMEM((2, LOCAL, NC, NY, NX, ROWS, D), BF16),
            pltpu.VMEM((2, LOCAL, NY, NX, ROWS, D), BF16),
            pltpu.VMEM((LOCAL, NX, ROWS, D), BF16),
            pltpu.VMEM((LOCAL, NX - 1, ROWS, D), BF16),
            pltpu.VMEM((LOCAL, ROWS, D), BF16),
            pltpu.VMEM((LOCAL, NX - 1, NY, ROWS, D), BF16),
            pltpu.VMEM((GROUPS,) + chunk, F32),
            pltpu.VMEM((GROUPS - 1,) + chunk, F32),
            pltpu.VMEM(chunk, F32),
            pltpu.VMEM(chunk, F32),
            pltpu.VMEM(chunk, F32),
            pltpu.VMEM(chunk, F32),
            pltpu.VMEM((NX,) + chunk, F32),
            pltpu.VMEM(chunk, F32),
            pltpu.VMEM((GROUPS,) + chunk, F32),
            dma((5,)), dma((GROUPS,)), dma((GROUPS,)), dma((GROUPS,)), dma((GROUPS,)),
            dma((2, LOCAL, 8)), dma((2, LOCAL, 8)), dma((2, LOCAL, 5)), dma((2, LOCAL, 5)),
            dma((20,)), dma((20,)),
        ],
        compiler_params=pltpu.CompilerParams(
            collective_id=0, has_side_effects=True, vmem_limit_bytes=56 * 2**20
        ),
    )(tokens, slot_param, inner_weight, outer_weight, output_grad)


def solution(mesh):
    in_specs = (
        P(("dp", "expert"), None, None),
        P(),
        P("expert", "dp", None),
        P("expert", "dp", None),
        P(("dp", "expert"), None, None),
    )
    out_specs = (
        P(("dp", "expert"), None, None),
        P(),
        P("expert", "dp", None),
        P("expert", "dp", None),
    )
    return jax.shard_map(
        on_device, mesh=mesh, in_specs=in_specs, out_specs=out_specs, check_vma=False
    )
```

```python
import functools

import jax
import jax.numpy as jnp
from jax import lax
from jax.experimental import pallas as pl
from jax.experimental.pallas import tpu as pltpu
from jax.sharding import PartitionSpec as P

MESH = pl.DeviceIdType.MESH
F32 = jnp.float32
BF16 = jnp.bfloat16
NX, NY, NC = 4, 2, 2
GROUPS = 8
LOCAL = 4
IMGS = 2
SLOTS = GROUPS * LOCAL
ROWS = 16
BLOCKS = NC * NY * NX
D = 1280
PATCHES = 256
HIDDEN = 320
TILE = 256
STEPS = D // TILE


def dot(a, b, ca=1, cb=0):
    return lax.dot_general(a, b, (((ca,), (cb,)), ((), ())), preferred_element_type=F32)


def permutation(source_of):
    size = 2 * IMGS * SLOTS
    row = lax.broadcasted_iota(jnp.int32, (size, size), 0)
    column = lax.broadcasted_iota(jnp.int32, (size, size), 1)
    return jnp.where(column == source_of(row), 1.0, 0.0).astype(BF16)


def slots_to_messages(r):
    group, array, expert, image = r // 16, (r // 8) % 2, (r // 2) % 4, r % 2
    return array * 64 + image * 32 + group * 4 + expert


def messages_to_slots(r):
    array, image, group, expert = r // 64, (r // 32) % 2, (r // 4) % 8, r % 4
    return group * 16 + array * 8 + expert * 2 + image


def messages_to_blocks(r):
    array, expert, group, image = r // 64, (r // 16) % 4, (r // 2) % 8, r % 2
    return group * 16 + array * 8 + expert * 2 + image


def blocks_to_messages(r):
    group, array, expert, image = r // 16, (r // 8) % 2, (r // 2) % 4, r % 2
    return array * 64 + expert * 16 + group * 2 + image


def kernel(
    tokens, slot_param, inner, outer, cotangent,
    grad_tokens, grad_param, grad_inner, grad_outer,
    T, G, SP, WI, WO, DI, CO, X, MSG, MSG_IN, BACK, BACK_IN, FIN, SUMS,
    R, ACT, SCA, PART, SIB, RY0, RX0, RY1, RX1,
    PP, AR1, S1, AR2, S2, AR3, AR4, S4, GP,
    in_sem, a2a_s, a2a_r, back_s, back_r, ag_s, ag_r, rs_s, rs_r, ar_s, ar_r,
):
    dp, ex = lax.axis_index("dp"), lax.axis_index("expert")
    x, y, c = dp // 4, (dp // 2) % 2, dp % 2

    def at_dp(px, py, pc):
        return (px * 4 + py * 2 + pc, ex)

    def right(k):
        return (x + k) % NX

    def left(k):
        return (x + NX - k) % NX

    def to_x(k):
        return at_dp(right(k), y, c)

    to_y = at_dp(x, 1 - y, c)
    to_core = at_dp(x, y, 1 - c)

    def ex_to(k):
        return (ex + k) % GROUPS

    def ex_from(k):
        return (ex + GROUPS - k) % GROUPS

    def remote(src, dst, send, recv, device):
        return pltpu.make_async_remote_copy(
            src_ref=src, dst_ref=dst, send_sem=send, recv_sem=recv, device_id=device, device_id_type=MESH
        )

    barrier = pltpu.get_barrier_semaphore()
    for k in range(1, GROUPS):
        pl.semaphore_signal(barrier, inc=1, device_id=(dp, ex_to(k)), device_id_type=MESH)
    for k in range(1, NX):
        pl.semaphore_signal(barrier, inc=1, device_id=to_x(k), device_id_type=MESH)
    pl.semaphore_signal(barrier, inc=1, device_id=to_y, device_id_type=MESH)
    pl.semaphore_signal(barrier, inc=1, device_id=to_core, device_id_type=MESH)

    loads = [
        pltpu.make_async_copy(slot_param, SP, in_sem.at[0]),
        pltpu.make_async_copy(tokens, T, in_sem.at[1]),
        pltpu.make_async_copy(cotangent, G, in_sem.at[2]),
        pltpu.make_async_copy(inner, WI, in_sem.at[3]),
        pltpu.make_async_copy(outer, WO, in_sem.at[4]),
    ]
    for load in loads:
        load.start()
    for load in loads[:3]:
        load.wait()

    for i in range(IMGS):
        logits = dot(SP[...], T[i], 1, 1)
        ed = jnp.exp(logits - jnp.max(logits, axis=1, keepdims=True))
        dispatch = ed / jnp.sum(ed, axis=1, keepdims=True)
        ec = jnp.exp(logits - jnp.max(logits, axis=0, keepdims=True))
        combine = ec / jnp.sum(ec, axis=0, keepdims=True)
        DI[i] = dispatch
        CO[i] = combine
        X[i] = dot(dispatch.astype(BF16), T[i]).astype(BF16)
        X[IMGS + i] = dot(combine.astype(BF16), G[i]).astype(BF16)
    MSG[...] = (
        dot(permutation(slots_to_messages), X[...].reshape(2 * IMGS * SLOTS, D))
        .astype(BF16).reshape(GROUPS, ROWS, D)
    )

    pl.semaphore_wait(barrier, GROUPS - 1 + NX - 1 + 2)

    def a2a(k):
        return remote(MSG.at[ex_to(k)], MSG_IN.at[ex], a2a_s.at[k], a2a_r.at[k], (dp, ex_to(k)))

    for k in range(1, GROUPS):
        a2a(k).start()
    MSG_IN[ex] = MSG[ex]
    for k in range(1, GROUPS):
        a2a(k).wait_recv()
    blocks = (
        dot(permutation(messages_to_blocks), MSG_IN[...].reshape(2 * IMGS * SLOTS, D))
        .astype(BF16).reshape(2, LOCAL, ROWS, D)
    )
    for a in range(2):
        for e in range(LOCAL):
            R[a, e, c, y, x] = blocks[a, e]

    def block_copy(a, e, py, px, sem, device):
        ref = R.at[a, e, c, py, px]
        return remote(ref, ref, ag_s.at[a, e, sem], ag_r.at[a, e, sem], device)

    def gather_first(e, act):
        for k in range(1, NX):
            act(block_copy(0, e, y, x, k - 1, to_x(k)))
        act(block_copy(1, e, y, x, 3, to_y))
        for k in range(1, NX):
            act(block_copy(1, e, y, x, k - 1, to_x(k)))
        act(block_copy(0, e, y, x, 3, to_y))

    def gather_second_x(e, act, k):
        act(block_copy(1, e, 1 - y, x, 3 + k, to_x(k)))

    def gather_second_y(e, act, k):
        act(block_copy(0, e, y, left(k), 3 + k, to_y))

    def gather_third(e, act):
        for a in range(2):
            ref = R.at[a, e, c]
            act(remote(ref, ref, ag_s.at[a, e, 7], ag_r.at[a, e, 7], to_core))

    def start(copy):
        copy.start()

    def wait_send(copy):
        copy.wait_send()

    def wait_recv(a, e, sem):
        block_copy(a, e, y, x, sem, to_y).wait_recv()

    def second(e):
        wait_recv(1, e, 3)
        for k in range(1, NX):
            gather_second_x(e, start, k)
        for k in (1, 3, 2):
            wait_recv(0, e, k - 1)
            gather_second_y(e, start, k)

    def third(e):
        for sem in (0, 1, 2, 4, 5, 6):
            wait_recv(1, e, sem)
        for sem in (3, 4, 5, 6):
            wait_recv(0, e, sem)
        gather_third(e, start)

    def expert(e):
        for a in range(2):
            ref = R.at[a, e, c]
            remote(ref, ref, ag_s.at[a, e, 7], ag_r.at[a, e, 7], to_core).wait_recv()
        rows_in = R[0, e].reshape(BLOCKS * ROWS, D)
        rows_grad = R[1, e].reshape(BLOCKS * ROWS, D)
        hidden = dot(WI[e], rows_in, 1, 1)
        slope = dot(WO[e], rows_grad, 1, 1)
        phi = 0.5 * (1.0 + lax.erf(hidden * 0.7071067811865476))
        active = (hidden * phi).astype(BF16)
        scaled = (slope * (phi + hidden * jnp.exp(-0.5 * hidden * hidden) * 0.3989422804014327)).astype(BF16)
        active_t = active.T
        scaled_t = scaled.T
        for n in range(STEPS):
            cols = slice(n * TILE, (n + 1) * TILE)
            PART[0, e, :, :, :, :, cols] = (
                dot(active_t, WO[e, :, cols]).astype(BF16).reshape(NC, NY, NX, ROWS, TILE)
            )
            PART[1, e, :, :, :, :, cols] = (
                dot(scaled_t, WI[e, :, cols]).astype(BF16).reshape(NC, NY, NX, ROWS, TILE)
            )
        ACT[e] = active
        SCA[e] = scaled
        sums_core(e, start)

    def weight_grads(e):
        for n in range(STEPS):
            cols = slice(n * TILE, (n + 1) * TILE)
            rows_in = R[0, e, :, :, :, :, cols].reshape(BLOCKS * ROWS, TILE)
            rows_grad = R[1, e, :, :, :, :, cols].reshape(BLOCKS * ROWS, TILE)
            grad_outer[e, :, cols] = dot(ACT[e], rows_grad).astype(BF16)
            grad_inner[e, :, cols] = dot(SCA[e], rows_in).astype(BF16)

    def sum_copy(a, e, src, dst, sem, device):
        return remote(src, dst, rs_s.at[a, e, sem], rs_r.at[a, e, sem], device)

    def sums_core(e, act):
        for a in range(2):
            act(sum_copy(a, e, PART.at[a, e, 1 - c], SIB.at[a, e], 0, to_core))

    def sums_y0(e):
        return sum_copy(0, e, PART.at[0, e, c, 1 - y], RY0.at[e], 4, to_y)

    def sums_x0(e, k):
        return sum_copy(0, e, PART.at[0, e, c, y, right(k)], RX0.at[e, k - 1], k, to_x(k))

    def sums_x1(e, k):
        return sum_copy(1, e, PART.at[1, e, c, :, right(k)], RX1.at[e, k - 1], k, to_x(k))

    def sums_y1(e):
        return sum_copy(1, e, PART.at[1, e, c, 1 - y, x], RY1.at[e], 4, to_y)

    def add_core(e):
        for a in range(2):
            sum_copy(a, e, PART.at[a, e, 1 - c], SIB.at[a, e], 0, to_core).wait_recv()
        for a in range(2):
            PART[a, e, c] = (PART[a, e, c].astype(F32) + SIB[a, e].astype(F32)).astype(BF16)
            if a == 0:
                sums_y0(e).start()
            else:
                for k in range(1, NX):
                    sums_x1(e, k).start()

    def add_second(e):
        sums_y0(e).wait_recv()
        PART[0, e, c, y] = (PART[0, e, c, y].astype(F32) + RY0[e].astype(F32)).astype(BF16)
        for k in range(1, NX):
            sums_x0(e, k).start()
        total = PART[1, e, c, :, x].astype(F32)
        for k in range(1, NX):
            sums_x1(e, k).wait_recv()
            total = total + RX1[e, k - 1].astype(F32)
        PART[1, e, c, :, x] = total.astype(BF16)
        sums_y1(e).start()

    def add_third(e):
        total = PART[0, e, c, y, x].astype(F32)
        for k in range(1, NX):
            sums_x0(e, k).wait_recv()
            total = total + RX0[e, k - 1].astype(F32)
        FIN[0, e] = total.astype(BF16)
        sums_y1(e).wait_recv()
        FIN[1, e] = (PART[1, e, c, y, x].astype(F32) + RY1[e].astype(F32)).astype(BF16)

    gather_first(0, start)
    gather_first(1, start)
    for load in loads[3:]:
        load.wait()

    def step(t, carry):
        def stage(lag, work):
            @pl.when(jnp.logical_and(t >= lag, t < LOCAL + lag))
            def _():
                work(t - lag)

        stage(0, second)
        stage(-2, lambda e: gather_first(e, start))
        stage(1, third)
        stage(3, add_core)
        stage(4, add_second)
        stage(5, add_third)
        stage(2, expert)
        stage(6, weight_grads)
        return carry

    lax.fori_loop(0, LOCAL + 5, step, 0)

    BACK[...] = (
        dot(permutation(blocks_to_messages), FIN[...].reshape(2 * IMGS * SLOTS, D))
        .astype(BF16).reshape(GROUPS, ROWS, D)
    )

    def back(k):
        return remote(BACK.at[ex_to(k)], BACK_IN.at[ex], back_s.at[k], back_r.at[k], (dp, ex_to(k)))

    for k in range(1, GROUPS):
        back(k).start()
    BACK_IN[ex] = BACK[ex]
    weight_grads(LOCAL - 1)
    for k in range(1, GROUPS):
        back(k).wait_recv()
    SUMS[...] = (
        dot(permutation(messages_to_slots), BACK_IN[...].reshape(2 * IMGS * SLOTS, D))
        .astype(BF16).reshape(2, IMGS, SLOTS, D)
    )

    param = jnp.zeros((SLOTS, D), F32)
    logit_grads = []
    for i in range(IMGS):
        dispatch, combine = DI[i], CO[i]
        combine_grad = dot(SUMS[0, i], G[i], 1, 1)
        dispatch_grad = dot(SUMS[1, i], T[i], 1, 1)
        combine_term = combine * (combine_grad - jnp.sum(combine * combine_grad, axis=0, keepdims=True))
        dispatch_term = dispatch * (dispatch_grad - jnp.sum(dispatch * dispatch_grad, axis=1, keepdims=True))
        logit_grad = (combine_term + dispatch_term).astype(BF16)
        logit_grads.append(logit_grad)
        param = param + dot(logit_grad, T[i])

    for j in range(GROUPS):
        PP[j] = param[8 * (j // 2):8 * (j // 2) + 8, 640 * (j % 2):640 * (j % 2) + 640]

    def ar_scatter(k):
        return remote(PP.at[ex_to(k)], AR1.at[k - 1], ar_s.at[k], ar_r.at[k], (dp, ex_to(k)))

    for k in range(1, GROUPS):
        ar_scatter(k).start()

    for i in range(IMGS):
        both = jnp.concatenate([DI[i].astype(BF16), logit_grads[i]], axis=0)
        rows = jnp.concatenate([SUMS[1, i], SP[...]], axis=0)
        grad_tokens[i] = dot(both.T, rows).astype(BF16)

    total = PP[ex]
    for k in range(1, GROUPS):
        ar_scatter(k).wait_recv()
        total = total + AR1[k - 1]
    S1[...] = total
    ar_core = remote(S1, AR2, ar_s.at[8], ar_r.at[8], to_core)
    ar_core.start()
    ar_core.wait_recv()
    S2[...] = S1[...] + AR2[...]
    ar_y = remote(S2, AR3, ar_s.at[9], ar_r.at[9], to_y)
    ar_y.start()
    ar_y.wait_recv()
    AR4[x] = S2[...] + AR3[...]

    def ar_x(k):
        return remote(AR4.at[x], AR4.at[x], ar_s.at[9 + k], ar_r.at[9 + k], to_x(k))

    for k in range(1, NX):
        ar_x(k).start()
    for k in range(1, NX):
        ar_x(k).wait_recv()
    GP[ex] = (AR4[0] + AR4[1]) + (AR4[2] + AR4[3])

    def ar_gather(k):
        return remote(GP.at[ex], GP.at[ex], ar_s.at[12 + k], ar_r.at[12 + k], (dp, ex_to(k)))

    for k in range(1, GROUPS):
        ar_gather(k).start()

    def drain(e, carry):
        gather_first(e, wait_send)
        for k in range(1, NX):
            gather_second_x(e, wait_send, k)
            gather_second_y(e, wait_send, k)
            sums_x0(e, k).wait_send()
            sums_x1(e, k).wait_send()
        gather_third(e, wait_send)
        sums_core(e, wait_send)
        sums_y0(e).wait_send()
        sums_y1(e).wait_send()
        return carry

    lax.fori_loop(0, LOCAL, drain, 0)
    for k in range(1, GROUPS):
        a2a(k).wait_send()
        back(k).wait_send()
        ar_scatter(k).wait_send()
    ar_core.wait_send()
    ar_y.wait_send()
    for k in range(1, NX):
        ar_x(k).wait_send()
    for k in range(1, GROUPS):
        ar_gather(k).wait_recv()
    for k in range(1, GROUPS):
        ar_gather(k).wait_send()
    for j in range(GROUPS):
        grad_param[8 * (j // 2):8 * (j // 2) + 8, 640 * (j % 2):640 * (j % 2) + 640] = GP[j]


def write_out(*refs):
    copies = [pltpu.make_async_copy(refs[i], refs[4 + i], refs[8].at[i]) for i in range(4)]
    for copy in copies:
        copy.start()
    for copy in copies:
        copy.wait()


def on_device(tokens, slot_param, inner_weight, outer_weight, output_grad):
    vmem = pl.BlockSpec(memory_space=pltpu.VMEM)
    chunk = (8, D * SLOTS // (8 * GROUPS))
    dma = pltpu.SemaphoreType.DMA
    results = pl.pallas_call(
        kernel,
        out_shape=(
            pltpu.VMEM(tokens.shape, BF16),
            pltpu.VMEM(slot_param.shape, F32),
            pltpu.VMEM(inner_weight.shape, BF16),
            pltpu.VMEM(outer_weight.shape, BF16),
        ),
        in_specs=[pl.BlockSpec(memory_space=pltpu.HBM)] * 5,
        out_specs=(vmem,) * 4,
        scratch_shapes=[
            pltpu.VMEM((IMGS, PATCHES, D), BF16),
            pltpu.VMEM((IMGS, PATCHES, D), BF16),
            pltpu.VMEM((SLOTS, D), BF16),
            pltpu.VMEM((LOCAL, HIDDEN, D), BF16),
            pltpu.VMEM((LOCAL, HIDDEN, D), BF16),
            pltpu.VMEM((IMGS, SLOTS, PATCHES), F32),
            pltpu.VMEM((IMGS, SLOTS, PATCHES), F32),
            pltpu.VMEM((2 * IMGS, SLOTS, D), BF16),
            pltpu.VMEM((GROUPS, ROWS, D), BF16),
            pltpu.VMEM((GROUPS, ROWS, D), BF16),
            pltpu.VMEM((GROUPS, ROWS, D), BF16),
            pltpu.VMEM((GROUPS, ROWS, D), BF16),
            pltpu.VMEM((2, LOCAL, ROWS, D), BF16),
            pltpu.VMEM((2, IMGS, SLOTS, D), BF16),
            pltpu.VMEM((2, LOCAL, NC, NY, NX, ROWS, D), BF16),
            pltpu.VMEM((LOCAL, HIDDEN, BLOCKS * ROWS), BF16),
            pltpu.VMEM((LOCAL, HIDDEN, BLOCKS * ROWS), BF16),
            pltpu.VMEM((2, LOCAL, NC, NY, NX, ROWS, D), BF16),
            pltpu.VMEM((2, LOCAL, NY, NX, ROWS, D), BF16),
            pltpu.VMEM((LOCAL, NX, ROWS, D), BF16),
            pltpu.VMEM((LOCAL, NX - 1, ROWS, D), BF16),
            pltpu.VMEM((LOCAL, ROWS, D), BF16),
            pltpu.VMEM((LOCAL, NX - 1, NY, ROWS, D), BF16),
            pltpu.VMEM((GROUPS,) + chunk, F32),
            pltpu.VMEM((GROUPS - 1,) + chunk, F32),
            pltpu.VMEM(chunk, F32),
            pltpu.VMEM(chunk, F32),
            pltpu.VMEM(chunk, F32),
            pltpu.VMEM(chunk, F32),
            pltpu.VMEM((NX,) + chunk, F32),
            pltpu.VMEM(chunk, F32),
            pltpu.VMEM((GROUPS,) + chunk, F32),
            dma((5,)), dma((GROUPS,)), dma((GROUPS,)), dma((GROUPS,)), dma((GROUPS,)),
            dma((2, LOCAL, 8)), dma((2, LOCAL, 8)), dma((2, LOCAL, 5)), dma((2, LOCAL, 5)),
            dma((20,)), dma((20,)),
        ],
        compiler_params=pltpu.CompilerParams(
            collective_id=0, has_side_effects=True, vmem_limit_bytes=54 * 2**20
        ),
    )(tokens, slot_param, inner_weight, outer_weight, output_grad)
    return pl.pallas_call(
        write_out,
        out_shape=tuple(jax.ShapeDtypeStruct(result.shape, result.dtype) for result in results),
        in_specs=[vmem] * 4,
        out_specs=(pl.BlockSpec(memory_space=pltpu.HBM),) * 4,
        scratch_shapes=[dma((4,))],
        compiler_params=pltpu.CompilerParams(vmem_limit_bytes=2**20),
    )(*[pltpu.with_memory_space_constraint(result, pltpu.VMEM) for result in results])


def solution(mesh):
    in_specs = (
        P(("dp", "expert"), None, None),
        P(),
        P("expert", "dp", None),
        P("expert", "dp", None),
        P(("dp", "expert"), None, None),
    )
    out_specs = (
        P(("dp", "expert"), None, None),
        P(),
        P("expert", "dp", None),
        P("expert", "dp", None),
    )
    return jax.shard_map(
        on_device, mesh=mesh, in_specs=in_specs, out_specs=out_specs, check_vma=False
    )
```

```python
import functools

import jax
import jax.numpy as jnp
from jax import lax
from jax.experimental import pallas as pl
from jax.experimental.pallas import tpu as pltpu
from jax.sharding import PartitionSpec as P

MESH = pl.DeviceIdType.MESH
F32 = jnp.float32
BF16 = jnp.bfloat16
NX, NY, NC = 4, 2, 2
NH, NZ = 2, 4
GROUPS = NH * NZ
LOCAL = 4
IMGS = 2
SLOTS = GROUPS * LOCAL
ROWS = 16
BLOCKS = NC * NY * NX
D = 1280
PATCHES = 256
HIDDEN = 320
TILE = 256
STEPS = D // TILE

ORDER = (
    "G00 G10 G02 G11",
    "G13 G01 S00 G12",
    "S02 S10 G03 T00",
    "S11 S12 S01 X00",
    "O10 S13 T02 C00",
    "O11 O12 T10 S03",
    "X02 T01 X10 T12",
    "C02 O13 T11 X01",
    "C10 X12 D00 X11",
    "C01 C12 T03 C11",
    "T13 D10 X03 X13",
    "D02 C13 C03 D12",
    "E10 D11 E00 D13",
    "D01 D03 E02 F10",
    "E11 E12 E13 E01",
    "F12 F13 F11 E03",
)


def dot(a, b, ca=1, cb=0):
    return lax.dot_general(a, b, (((ca,), (cb,)), ((), ())), preferred_element_type=F32)


def permutation(source_of):
    size = 2 * IMGS * SLOTS
    row = lax.broadcasted_iota(jnp.int32, (size, size), 0)
    column = lax.broadcasted_iota(jnp.int32, (size, size), 1)
    return jnp.where(column == source_of(row), 1.0, 0.0).astype(BF16)


def slots_to_messages(r):
    group, array, expert, image = r // 16, (r // 8) % 2, (r // 2) % 4, r % 2
    return array * 64 + image * 32 + group * 4 + expert


def messages_to_slots(r):
    array, image, group, expert = r // 64, (r // 32) % 2, (r // 4) % 8, r % 4
    return group * 16 + array * 8 + expert * 2 + image


def messages_to_blocks(r):
    array, expert, group, image = r // 64, (r // 16) % 4, (r // 2) % 8, r % 2
    return group * 16 + array * 8 + expert * 2 + image


def blocks_to_messages(r):
    group, array, expert, image = r // 16, (r // 8) % 2, (r // 2) % 4, r % 2
    return array * 64 + expert * 16 + group * 2 + image


def kernel(
    tokens, slot_param, inner, outer, cotangent,
    grad_tokens, grad_param, grad_inner, grad_outer,
    T, G, SP, WI, WO, DI, CO, X, MSG, MSG_IN, BACK, BACK_IN, FIN, SUMS,
    R, ACT, SCA, SLOPE, PART, SIB, RY0, RX0, RY1, RX1,
    PP, AR1, AR2, GP,
    in_sem, a2a_s, a2a_r, back_s, back_r, ag_s, ag_r, rs_s, rs_r, ar_s, ar_r, mid_s, mid_r, last_s, last_r,
):
    dp, ex = lax.axis_index("dp"), lax.axis_index("expert")
    x, y, c = dp // 4, (dp // 2) % 2, dp % 2
    h, z = ex // NZ, ex % NZ

    def at_dp(px, py, pc):
        return (px * 4 + py * 2 + pc, ex)

    def right(k):
        return (x + k) % NX

    def left(k):
        return (x + NX - k) % NX

    def to_x(k):
        return at_dp(right(k), y, c)

    to_y = at_dp(x, 1 - y, c)
    to_core = at_dp(x, y, 1 - c)

    def ex_to(k):
        return (ex + k) % GROUPS

    def ex_from(k):
        return (ex + GROUPS - k) % GROUPS

    def remote(src, dst, send, recv, device):
        return pltpu.make_async_remote_copy(
            src_ref=src, dst_ref=dst, send_sem=send, recv_sem=recv, device_id=device, device_id_type=MESH
        )

    member = c * NZ + z
    plane = (x * NY + y) * NH + h

    def to_member(k):
        other = (member + k) % GROUPS
        return other, ((x * NY + y) * NC + other // NZ, h * NZ + other % NZ)

    def to_plane(k):
        other = (plane + k) % (NX * NY * NH)
        return (other // NH * NC + c, other % NH * NZ + z)

    barrier = pltpu.get_barrier_semaphore()
    partners = [(dp, ex_to(k)) for k in range(1, GROUPS)] + [to_core]
    partners += [(at_dp(x, y, 1 - c)[0], h * NZ + (z + k) % NZ) for k in range(1, NZ)]
    partners += [
        (at_dp(right(dx), (y + dy) % NY, c)[0], (h + dh) % NH * NZ + z)
        for dx in range(NX) for dy in range(NY) for dh in range(NH) if dx or dy
    ]
    for partner in partners:
        pl.semaphore_signal(barrier, inc=1, device_id=partner, device_id_type=MESH)

    loads = [
        pltpu.make_async_copy(slot_param, SP, in_sem.at[0]),
        pltpu.make_async_copy(tokens, T, in_sem.at[1]),
        pltpu.make_async_copy(cotangent, G, in_sem.at[2]),
        pltpu.make_async_copy(inner, WI, in_sem.at[3]),
        pltpu.make_async_copy(outer, WO, in_sem.at[4]),
    ]
    for load in loads:
        load.start()
    for load in loads[:3]:
        load.wait()

    for i in range(IMGS):
        logits = dot(SP[...], T[i], 1, 1)
        ed = jnp.exp(logits - jnp.max(logits, axis=1, keepdims=True))
        dispatch = ed / jnp.sum(ed, axis=1, keepdims=True)
        ec = jnp.exp(logits - jnp.max(logits, axis=0, keepdims=True))
        combine = ec / jnp.sum(ec, axis=0, keepdims=True)
        DI[i] = dispatch
        CO[i] = combine
        X[i] = dot(dispatch.astype(BF16), T[i]).astype(BF16)
        X[IMGS + i] = dot(combine.astype(BF16), G[i]).astype(BF16)
    MSG[...] = (
        dot(permutation(slots_to_messages), X[...].reshape(2 * IMGS * SLOTS, D))
        .astype(BF16).reshape(GROUPS, ROWS, D)
    )

    pl.semaphore_wait(barrier, len(partners))

    def a2a(k):
        return remote(MSG.at[ex_to(k)], MSG_IN.at[ex], a2a_s.at[k], a2a_r.at[k], (dp, ex_to(k)))

    for k in range(1, GROUPS):
        a2a(k).start()
    MSG_IN[ex] = MSG[ex]
    for k in range(1, GROUPS):
        a2a(k).wait_recv()
    blocks = (
        dot(permutation(messages_to_blocks), MSG_IN[...].reshape(2 * IMGS * SLOTS, D))
        .astype(BF16).reshape(2, LOCAL, ROWS, D)
    )
    for a in range(2):
        for e in range(LOCAL):
            R[a, e, c, y, x] = blocks[a, e]

    def block_copy(a, e, py, px, sem, device):
        ref = R.at[a, e, c, py, px]
        return remote(ref, ref, ag_s.at[a, e, sem], ag_r.at[a, e, sem], device)

    def gather_first(a, e, act):
        if a == 1:
            act(block_copy(1, e, y, x, 3, to_y))
        for k in range(1, NX) if a == 0 else (1, 3):
            act(block_copy(a, e, y, x, k - 1, to_x(k)))
        if a == 0:
            act(block_copy(0, e, y, x, 3, to_y))

    def gather_second_x(e, act, k):
        act(block_copy(1, e, 1 - y, x, 3 + k, to_x(k)))

    def gather_second_y(e, act, k):
        act(block_copy(0, e, y, left(k), 3 + k, to_y))

    def gather_on_right(e, act):
        act(block_copy(1, e, y, left(1), 1, to_x(1)))

    def gather_on_left(e, act):
        act(block_copy(1, e, 1 - y, right(1), 5, to_x(3)))

    def gather_third(a, e):
        ref = R.at[a, e, c]
        return remote(ref, ref, ag_s.at[a, e, 7], ag_r.at[a, e, 7], to_core)

    def start(copy):
        copy.start()

    def wait_send(copy):
        copy.wait_send()

    def wait_recv(a, e, sem):
        block_copy(a, e, y, x, sem, to_y).wait_recv()

    def second(a, e):
        if a == 0:
            for k in (1, 3, 2):
                wait_recv(0, e, k - 1)
                gather_second_y(e, start, k)
        else:
            wait_recv(1, e, 3)
            for k in (1, 3):
                gather_second_x(e, start, k)
            wait_recv(1, e, 0)
            gather_on_right(e, start)

    def second_on(a, e):
        wait_recv(1, e, 6)
        gather_on_left(e, start)

    def third(a, e):
        for sem in (3, 4, 5, 6) if a == 0 else (2, 1, 4, 5):
            wait_recv(a, e, sem)
        gather_third(a, e).start()

    def expert(a, e):
        gather_third(a, e).wait_recv()
        rows = R[a, e].reshape(BLOCKS * ROWS, D)
        if a == 0:
            hidden = dot(WI[e], rows, 1, 1)
            phi = 0.5 * (1.0 + lax.erf(hidden * 0.7071067811865476))
            SLOPE[e] = phi + hidden * jnp.exp(-0.5 * hidden * hidden) * 0.3989422804014327
            act, kept, weight = (hidden * phi).astype(BF16), ACT, WO
        else:
            act, kept, weight = (dot(WO[e], rows, 1, 1) * SLOPE[e]).astype(BF16), SCA, WI
        kept[e] = act
        act_t = act.T
        for n in range(STEPS):
            cols = slice(n * TILE, (n + 1) * TILE)
            PART[a, e, :, :, :, :, cols] = (
                dot(act_t, weight[e, :, cols]).astype(BF16).reshape(NC, NY, NX, ROWS, TILE)
            )
        sums_core(a, e).start()

    def weight_grads(e):
        for n in range(STEPS):
            cols = slice(n * TILE, (n + 1) * TILE)
            rows_in = R[0, e, :, :, :, :, cols].reshape(BLOCKS * ROWS, TILE)
            rows_grad = R[1, e, :, :, :, :, cols].reshape(BLOCKS * ROWS, TILE)
            grad_outer[e, :, cols] = dot(ACT[e], rows_grad).astype(BF16)
            grad_inner[e, :, cols] = dot(SCA[e], rows_in).astype(BF16)

    def sum_copy(a, e, src, dst, sem, device):
        return remote(src, dst, rs_s.at[a, e, sem], rs_r.at[a, e, sem], device)

    def sums_core(a, e):
        return sum_copy(a, e, PART.at[a, e, 1 - c], SIB.at[a, e], 0, to_core)

    def sums_y0(e):
        return sum_copy(0, e, PART.at[0, e, c, 1 - y], RY0.at[e], 4, to_y)

    def sums_x0(e, k):
        return sum_copy(0, e, PART.at[0, e, c, y, right(k)], RX0.at[e, k - 1], k, to_x(k))

    def sums_x1(e, k):
        return sum_copy(1, e, PART.at[1, e, c, :, right(k)], RX1.at[e, k - 1], k, to_x(k))

    def sums_on_right(e):
        return sum_copy(1, e, PART.at[1, e, c, y, right(2)], RX1.at[e, 1, 0], 2, to_x(1))

    def sums_on_left(e):
        return sum_copy(1, e, PART.at[1, e, c, 1 - y, right(2)], RX1.at[e, 1, 1], 5, to_x(3))

    def sums_y1(e):
        return sum_copy(1, e, PART.at[1, e, c, 1 - y, x], RY1.at[e], 4, to_y)

    def add(a, b):
        return (a.astype(F32) + b.astype(F32)).astype(BF16)

    def add_core(a, e):
        sums_core(a, e).wait_recv()
        PART[a, e, c] = add(PART[a, e, c], SIB[a, e])
        if a == 0:
            sums_y0(e).start()
        else:
            sums_on_right(e).start()
            sums_on_left(e).start()

    def add_second(a, e):
        if a == 0:
            sums_y0(e).wait_recv()
            PART[0, e, c, y] = add(PART[0, e, c, y], RY0[e])
            for k in range(1, NX):
                sums_x0(e, k).start()
        else:
            sums_on_right(e).wait_recv()
            PART[1, e, c, y, right(1)] = add(PART[1, e, c, y, right(1)], RX1[e, 1, 0])
            sums_on_left(e).wait_recv()
            PART[1, e, c, 1 - y, left(1)] = add(PART[1, e, c, 1 - y, left(1)], RX1[e, 1, 1])
            for k in (1, 3):
                sums_x1(e, k).start()

    def add_third(a, e):
        if a == 0:
            total = PART[0, e, c, y, x].astype(F32)
            for k in range(1, NX):
                sums_x0(e, k).wait_recv()
                total = total + RX0[e, k - 1].astype(F32)
            FIN[0, e] = total.astype(BF16)
        else:
            total = PART[1, e, c, :, x].astype(F32)
            for k in (1, 3):
                sums_x1(e, k).wait_recv()
                total = total + RX1[e, k - 1].astype(F32)
            PART[1, e, c, :, x] = total.astype(BF16)
            sums_y1(e).start()

    def add_fourth(a, e):
        sums_y1(e).wait_recv()
        FIN[1, e] = add(PART[1, e, c, y, x], RY1[e])

    for load in loads[3:]:
        load.wait()
    steps = {
        "G": lambda a, e: gather_first(a, e, start), "S": second, "O": second_on, "T": third, "X": expert,
        "C": add_core, "D": add_second, "E": add_third, "F": add_fourth,
    }
    for line in ORDER:
        for word in line.split():
            steps[word[0]](int(word[1]), int(word[2]))

    BACK[...] = (
        dot(permutation(blocks_to_messages), FIN[...].reshape(2 * IMGS * SLOTS, D))
        .astype(BF16).reshape(GROUPS, ROWS, D)
    )

    def back(k):
        return remote(BACK.at[ex_to(k)], BACK_IN.at[ex], back_s.at[k], back_r.at[k], (dp, ex_to(k)))

    for k in range(1, GROUPS):
        back(k).start()
    BACK_IN[ex] = BACK[ex]

    def grads(e, carry):
        weight_grads(e)
        return carry

    lax.fori_loop(0, LOCAL, grads, 0)
    for k in range(1, GROUPS):
        back(k).wait_recv()
    SUMS[...] = (
        dot(permutation(messages_to_slots), BACK_IN[...].reshape(2 * IMGS * SLOTS, D))
        .astype(BF16).reshape(2, IMGS, SLOTS, D)
    )

    param = jnp.zeros((SLOTS, D), F32)
    logit_grads = []
    for i in range(IMGS):
        dispatch, combine = DI[i], CO[i]
        combine_grad = dot(SUMS[0, i], G[i], 1, 1)
        dispatch_grad = dot(SUMS[1, i], T[i], 1, 1)
        combine_term = combine * (combine_grad - jnp.sum(combine * combine_grad, axis=0, keepdims=True))
        dispatch_term = dispatch * (dispatch_grad - jnp.sum(dispatch * dispatch_grad, axis=1, keepdims=True))
        logit_grad = (combine_term + dispatch_term).astype(BF16)
        logit_grads.append(logit_grad)
        param = param + dot(logit_grad, T[i])

    for j in range(GROUPS):
        PP[j] = param[8 * (j // 2):8 * (j // 2) + 8, 640 * (j % 2):640 * (j % 2) + 640]

    def ar_scatter(k):
        other, device = to_member(k)
        return remote(PP.at[other], AR1.at[k - 1], ar_s.at[k], ar_r.at[k], device)

    def ar_plane(k):
        return remote(AR2.at[plane], AR2.at[plane], mid_s.at[k], mid_r.at[k], to_plane(k))

    def ar_gather(k):
        return remote(GP.at[member], GP.at[member], last_s.at[k], last_r.at[k], to_member(k)[1])

    for k in range(1, GROUPS):
        ar_scatter(k).start()

    for i in range(IMGS):
        both = jnp.concatenate([DI[i].astype(BF16), logit_grads[i]], axis=0)
        rows = jnp.concatenate([SUMS[1, i], SP[...]], axis=0)
        grad_tokens[i] = dot(both.T, rows).astype(BF16)

    total = PP[member]
    for k in range(1, GROUPS):
        ar_scatter(k).wait_recv()
        total = total + AR1[k - 1]
    AR2[plane] = total
    for k in range(1, NX * NY * NH):
        ar_plane(k).start()
    for k in range(1, NX * NY * NH):
        ar_plane(k).wait_recv()
    total = AR2[0]
    for k in range(1, NX * NY * NH):
        total = total + AR2[k]
    GP[member] = total
    for k in range(1, GROUPS):
        ar_gather(k).start()

    def drain(e, carry):
        for a in range(2):
            gather_first(a, e, wait_send)
            gather_third(a, e).wait_send()
            sums_core(a, e).wait_send()
        gather_on_right(e, wait_send)
        gather_on_left(e, wait_send)
        for k in range(1, NX):
            gather_second_y(e, wait_send, k)
            sums_x0(e, k).wait_send()
        for k in (1, 3):
            gather_second_x(e, wait_send, k)
            sums_x1(e, k).wait_send()
        sums_on_right(e).wait_send()
        sums_on_left(e).wait_send()
        sums_y0(e).wait_send()
        sums_y1(e).wait_send()
        return carry

    lax.fori_loop(0, LOCAL, drain, 0)
    for k in range(1, GROUPS):
        a2a(k).wait_send()
        back(k).wait_send()
        ar_scatter(k).wait_send()
    for k in range(1, NX * NY * NH):
        ar_plane(k).wait_send()
    for k in range(1, GROUPS):
        ar_gather(k).wait_recv()
    for k in range(1, GROUPS):
        ar_gather(k).wait_send()
    for j in range(GROUPS):
        grad_param[8 * (j // 2):8 * (j // 2) + 8, 640 * (j % 2):640 * (j % 2) + 640] = GP[j]


def write_out(*refs):
    copies = [pltpu.make_async_copy(refs[i], refs[4 + i], refs[8].at[i]) for i in range(4)]
    for copy in copies:
        copy.start()
    for copy in copies:
        copy.wait()


def on_device(tokens, slot_param, inner_weight, outer_weight, output_grad):
    vmem = pl.BlockSpec(memory_space=pltpu.VMEM)
    chunk = (8, D * SLOTS // (8 * GROUPS))
    dma = pltpu.SemaphoreType.DMA
    results = pl.pallas_call(
        kernel,
        out_shape=(
            pltpu.VMEM(tokens.shape, BF16),
            pltpu.VMEM(slot_param.shape, F32),
            pltpu.VMEM(inner_weight.shape, BF16),
            pltpu.VMEM(outer_weight.shape, BF16),
        ),
        in_specs=[pl.BlockSpec(memory_space=pltpu.HBM)] * 5,
        out_specs=(vmem,) * 4,
        scratch_shapes=[
            pltpu.VMEM((IMGS, PATCHES, D), BF16),
            pltpu.VMEM((IMGS, PATCHES, D), BF16),
            pltpu.VMEM((SLOTS, D), BF16),
            pltpu.VMEM((LOCAL, HIDDEN, D), BF16),
            pltpu.VMEM((LOCAL, HIDDEN, D), BF16),
            pltpu.VMEM((IMGS, SLOTS, PATCHES), F32),
            pltpu.VMEM((IMGS, SLOTS, PATCHES), F32),
            pltpu.VMEM((2 * IMGS, SLOTS, D), BF16),
            pltpu.VMEM((GROUPS, ROWS, D), BF16),
            pltpu.VMEM((GROUPS, ROWS, D), BF16),
            pltpu.VMEM((GROUPS, ROWS, D), BF16),
            pltpu.VMEM((GROUPS, ROWS, D), BF16),
            pltpu.VMEM((2, LOCAL, ROWS, D), BF16),
            pltpu.VMEM((2, IMGS, SLOTS, D), BF16),
            pltpu.VMEM((2, LOCAL, NC, NY, NX, ROWS, D), BF16),
            pltpu.VMEM((LOCAL, HIDDEN, BLOCKS * ROWS), BF16),
            pltpu.VMEM((LOCAL, HIDDEN, BLOCKS * ROWS), BF16),
            pltpu.VMEM((LOCAL, HIDDEN, BLOCKS * ROWS), F32),
            pltpu.VMEM((2, LOCAL, NC, NY, NX, ROWS, D), BF16),
            pltpu.VMEM((2, LOCAL, NY, NX, ROWS, D), BF16),
            pltpu.VMEM((LOCAL, NX, ROWS, D), BF16),
            pltpu.VMEM((LOCAL, NX - 1, ROWS, D), BF16),
            pltpu.VMEM((LOCAL, ROWS, D), BF16),
            pltpu.VMEM((LOCAL, NX - 1, NY, ROWS, D), BF16),
            pltpu.VMEM((GROUPS,) + chunk, F32),
            pltpu.VMEM((GROUPS - 1,) + chunk, F32),
            pltpu.VMEM((NX * NY * NH,) + chunk, F32),
            pltpu.VMEM((GROUPS,) + chunk, F32),
            dma((5,)), dma((GROUPS,)), dma((GROUPS,)), dma((GROUPS,)), dma((GROUPS,)),
            dma((2, LOCAL, 8)), dma((2, LOCAL, 8)), dma((2, LOCAL, 6)), dma((2, LOCAL, 6)),
            dma((GROUPS,)), dma((GROUPS,)), dma((NX * NY * NH,)), dma((NX * NY * NH,)),
            dma((GROUPS,)), dma((GROUPS,)),
        ],
        compiler_params=pltpu.CompilerParams(
            collective_id=0, has_side_effects=True, vmem_limit_bytes=54 * 2**20
        ),
    )(tokens, slot_param, inner_weight, outer_weight, output_grad)
    return pl.pallas_call(
        write_out,
        out_shape=tuple(jax.ShapeDtypeStruct(result.shape, result.dtype) for result in results),
        in_specs=[vmem] * 4,
        out_specs=(pl.BlockSpec(memory_space=pltpu.HBM),) * 4,
        scratch_shapes=[dma((4,))],
        compiler_params=pltpu.CompilerParams(vmem_limit_bytes=2**20),
    )(*[pltpu.with_memory_space_constraint(result, pltpu.VMEM) for result in results])


def solution(mesh):
    in_specs = (
        P(("dp", "expert"), None, None),
        P(),
        P("expert", "dp", None),
        P("expert", "dp", None),
        P(("dp", "expert"), None, None),
    )
    out_specs = (
        P(("dp", "expert"), None, None),
        P(),
        P("expert", "dp", None),
        P("expert", "dp", None),
    )
    return jax.shard_map(
        on_device, mesh=mesh, in_specs=in_specs, out_specs=out_specs, check_vma=False
    )
```

```python
import functools

import jax
import jax.numpy as jnp
from jax import lax
from jax.experimental import pallas as pl
from jax.experimental.pallas import tpu as pltpu
from jax.sharding import PartitionSpec as P

MESH = pl.DeviceIdType.MESH
F32 = jnp.float32
BF16 = jnp.bfloat16
NX, NY, NC = 4, 2, 2
NH, NZ = 2, 4
GROUPS = NH * NZ
LOCAL = 4
IMGS = 2
SLOTS = GROUPS * LOCAL
ROWS = 16
BLOCKS = NC * NY * NX
D = 1280
PATCHES = 256
HIDDEN = 320
TILE = 256
STEPS = D // TILE
PARTS = 2
SLOT_ROWS = 2 * IMGS * SLOTS
SHARE = SLOTS * D // (8 * 128 * GROUPS)

ORDER = (
    "A00 G00 G11 G10",
    "G01 A01 G02 G12",
    "S00 S11 G13 S01",
    "S10 G03 T00 S12",
    "S02 O11 X00 O10",
    "T01 C00 S13 O12",
    "T11 X01 S03 T02",
    "T10 X11 O13 C01",
    "X02 T12 C11 X10",
    "D00 X12 C10 T03",
    "T13 C12 C02 D11",
    "X03 X13 D01 C03",
    "C13 D12 D10 E00",
    "D13 D02 D03 E10",
    "E11 E12 E13 E01",
    "F10 F11 B00 E02",
    "F12 E03 F13 B01",
)


def dot(a, b, ca=1, cb=0):
    return lax.dot_general(a, b, (((ca,), (cb,)), ((), ())), preferred_element_type=F32)


def place(rows, columns, source_of, part, half, transposed=False):
    shape = (columns, rows) if transposed else (rows, columns)
    row = lax.broadcasted_iota(jnp.int32, shape, 1 if transposed else 0)
    column = lax.broadcasted_iota(jnp.int32, shape, 0 if transposed else 1)
    source, in_half = source_of(row, part, half)
    return jnp.where(jnp.logical_and(column == source, in_half), 1.0, 0.0).astype(BF16)


def slots_of_message(r, part, half):
    group, array, expert, image = r // 16, (r // 4) % 2, (r // 2) % 2, r % 2
    return array * 64 + image * 32 + group * 4 + 2 * part + expert, (r // 8) % 2 == half


def message_of_blocks(r, part, half):
    array, expert, group, image = r // 32, (r // 16) % 2, (r // 2) % 8, r % 2
    return group * 16 + half * 8 + array * 4 + expert * 2 + image, r >= 0


def halves(array):
    return array[:, : D // 2], array[:, D // 2 :]


def kernel(
    tokens, slot_param, inner, outer, cotangent,
    grad_tokens, grad_param, grad_inner, grad_outer,
    T, G, SP, WI, WO, DI, CO, X, MSG, MSG_IN, BACK, BACK_IN, FIN, SUMS,
    R, ACT, SCA, SLOPE, PART, SIB, RY0, RX0, RY1, RX1,
    PP, AR1, AR2, GP,
    in_sem, a2a_s, a2a_r, back_s, back_r, ag_s, ag_r, rs_s, rs_r, ar_s, ar_r, mid_s, mid_r, last_s, last_r,
):
    dp, ex = lax.axis_index("dp"), lax.axis_index("expert")
    x, y, c = dp // 4, (dp // 2) % 2, dp % 2
    h, z = ex // NZ, ex % NZ

    def at_dp(px, py, pc):
        return (px * 4 + py * 2 + pc, ex)

    def right(k):
        return (x + k) % NX

    def left(k):
        return (x + NX - k) % NX

    def to_x(k):
        return at_dp(right(k), y, c)

    to_y = at_dp(x, 1 - y, c)
    to_core = at_dp(x, y, 1 - c)

    def ex_to(k):
        return (ex + k) % GROUPS

    def ex_from(k):
        return (ex + GROUPS - k) % GROUPS

    def remote(src, dst, send, recv, device):
        return pltpu.make_async_remote_copy(
            src_ref=src, dst_ref=dst, send_sem=send, recv_sem=recv, device_id=device, device_id_type=MESH
        )

    member = c * NZ + z
    plane = (x * NY + y) * NH + h

    def to_member(k):
        other = (member + k) % GROUPS
        return other, ((x * NY + y) * NC + other // NZ, h * NZ + other % NZ)

    def to_plane(k):
        other = (plane + k) % (NX * NY * NH)
        return (other // NH * NC + c, other % NH * NZ + z)

    barrier = pltpu.get_barrier_semaphore()
    partners = [
        (at_dp(right(dx), (y + dy) % NY, c)[0], (h + dh) % NH * NZ + z)
        for dx in (2, 1, 3, 0) for dh in (1, 0) for dy in (1, 0) if dx or dy
    ]
    partners += [(dp, ex_to(k)) for k in range(GROUPS - 1, 0, -1)]
    partners += [(at_dp(x, y, 1 - c)[0], h * NZ + (z + k) % NZ) for k in range(1, NZ)] + [to_core]
    for partner in partners:
        pl.semaphore_signal(barrier, inc=1, device_id=partner, device_id_type=MESH)

    loads = [
        pltpu.make_async_copy(slot_param, SP, in_sem.at[0]),
        pltpu.make_async_copy(tokens, T, in_sem.at[1]),
        pltpu.make_async_copy(cotangent, G, in_sem.at[2]),
        pltpu.make_async_copy(inner, WI, in_sem.at[3]),
        pltpu.make_async_copy(outer, WO, in_sem.at[4]),
    ]
    for load in loads:
        load.start()
    for load in loads[:3]:
        load.wait()

    for i in range(IMGS):
        logits = dot(SP[...], T[i], 1, 1)
        ed = jnp.exp(logits - jnp.max(logits, axis=1, keepdims=True))
        dispatch = ed / jnp.sum(ed, axis=1, keepdims=True)
        ec = jnp.exp(logits - jnp.max(logits, axis=0, keepdims=True))
        combine = ec / jnp.sum(ec, axis=0, keepdims=True)
        DI[i] = dispatch
        CO[i] = combine
        X[i] = dot(dispatch.astype(BF16), T[i]).astype(BF16)
        X[IMGS + i] = dot(combine.astype(BF16), G[i]).astype(BF16)
    flat = halves(X[...].reshape(SLOT_ROWS, D))
    for part in range(PARTS):
        rows = [dot(place(SLOT_ROWS, SLOT_ROWS, slots_of_message, part, j), flat[j]) for j in range(2)]
        MSG[part] = (rows[0] + rows[1]).astype(BF16).reshape(GROUPS, ROWS, D // 2)

    pl.semaphore_wait(barrier, len(partners))

    def a2a(part, k):
        return remote(
            MSG.at[part, ex_to(k)], MSG_IN.at[part, ex], a2a_s.at[part, k], a2a_r.at[part, k], (dp, ex_to(k))
        )

    for part in range(PARTS):
        for k in range(1, GROUPS):
            a2a(part, k).start()
    for part in range(PARTS):
        MSG_IN[part, ex] = MSG[part, ex]

    def arrive(a, part):
        for k in range(1, GROUPS):
            a2a(part, k).wait_recv()
        flat = MSG_IN[part].reshape(SLOT_ROWS, D // 2)
        for j in range(2):
            rows = dot(place(SLOT_ROWS // PARTS, SLOT_ROWS, message_of_blocks, part, j), flat).astype(BF16)
            rows = rows.reshape(2, LOCAL // PARTS, ROWS, D // 2)
            for a in range(2):
                for e in range(LOCAL // PARTS):
                    R[a, 2 * part + e, c, y, x, :, j * (D // 2):(j + 1) * (D // 2)] = rows[a, e]

    def block_copy(a, e, py, px, sem, device):
        ref = R.at[a, e, c, py, px]
        return remote(ref, ref, ag_s.at[a, e, sem], ag_r.at[a, e, sem], device)

    def gather_first(a, e, act):
        if a == 1:
            act(block_copy(1, e, y, x, 3, to_y))
        for k in range(1, NX) if a == 0 else (1, 3):
            act(block_copy(a, e, y, x, k - 1, to_x(k)))
        if a == 0:
            act(block_copy(0, e, y, x, 3, to_y))

    def gather_second_x(e, act, k):
        act(block_copy(1, e, 1 - y, x, 3 + k, to_x(k)))

    def gather_second_y(e, act, k):
        act(block_copy(0, e, y, left(k), 3 + k, to_y))

    def gather_on_right(e, act):
        act(block_copy(1, e, y, left(1), 1, to_x(1)))

    def gather_on_left(e, act):
        act(block_copy(1, e, 1 - y, right(1), 5, to_x(3)))

    def gather_third(a, e):
        ref = R.at[a, e, c]
        return remote(ref, ref, ag_s.at[a, e, 7], ag_r.at[a, e, 7], to_core)

    def start(copy):
        copy.start()

    def wait_send(copy):
        copy.wait_send()

    def wait_recv(a, e, sem):
        block_copy(a, e, y, x, sem, to_y).wait_recv()

    def second(a, e):
        if a == 0:
            for k in (1, 3, 2):
                wait_recv(0, e, k - 1)
                gather_second_y(e, start, k)
        else:
            wait_recv(1, e, 3)
            for k in (1, 3):
                gather_second_x(e, start, k)
            wait_recv(1, e, 0)
            gather_on_right(e, start)

    def second_on(a, e):
        wait_recv(1, e, 6)
        gather_on_left(e, start)

    def third(a, e):
        for sem in (3, 4, 5, 6) if a == 0 else (2, 1, 4, 5):
            wait_recv(a, e, sem)
        gather_third(a, e).start()

    def expert(a, e):
        gather_third(a, e).wait_recv()
        rows = R[a, e].reshape(BLOCKS * ROWS, D)
        if a == 0:
            hidden = dot(WI[e], rows, 1, 1)
            phi = 0.5 * (1.0 + lax.erf(hidden * 0.7071067811865476))
            SLOPE[e] = phi + hidden * jnp.exp(-0.5 * hidden * hidden) * 0.3989422804014327
            act, kept, weight = (hidden * phi).astype(BF16), ACT, WO
        else:
            act, kept, weight = (dot(WO[e], rows, 1, 1) * SLOPE[e]).astype(BF16), SCA, WI
        kept[e] = act
        act_t = act.T
        for n in range(STEPS):
            cols = slice(n * TILE, (n + 1) * TILE)
            PART[a, e, :, :, :, :, cols] = (
                dot(act_t, weight[e, :, cols]).astype(BF16).reshape(NC, NY, NX, ROWS, TILE)
            )
        sums_core(a, e).start()

    def weight_grads(e):
        for n in range(STEPS):
            cols = slice(n * TILE, (n + 1) * TILE)
            rows_in = R[0, e, :, :, :, :, cols].reshape(BLOCKS * ROWS, TILE)
            rows_grad = R[1, e, :, :, :, :, cols].reshape(BLOCKS * ROWS, TILE)
            grad_outer[e, :, cols] = dot(ACT[e], rows_grad).astype(BF16)
            grad_inner[e, :, cols] = dot(SCA[e], rows_in).astype(BF16)

    def sum_copy(a, e, src, dst, sem, device):
        return remote(src, dst, rs_s.at[a, e, sem], rs_r.at[a, e, sem], device)

    def sums_core(a, e):
        return sum_copy(a, e, PART.at[a, e, 1 - c], SIB.at[a, e], 0, to_core)

    def sums_y0(e):
        return sum_copy(0, e, PART.at[0, e, c, 1 - y], RY0.at[e], 4, to_y)

    def sums_x0(e, k):
        return sum_copy(0, e, PART.at[0, e, c, y, right(k)], RX0.at[e, k - 1], k, to_x(k))

    def sums_x1(e, k):
        return sum_copy(1, e, PART.at[1, e, c, :, right(k)], RX1.at[e, k - 1], k, to_x(k))

    def sums_on_right(e):
        return sum_copy(1, e, PART.at[1, e, c, y, right(2)], RX1.at[e, 1, 0], 2, to_x(1))

    def sums_on_left(e):
        return sum_copy(1, e, PART.at[1, e, c, 1 - y, right(2)], RX1.at[e, 1, 1], 5, to_x(3))

    def sums_y1(e):
        return sum_copy(1, e, PART.at[1, e, c, 1 - y, x], RY1.at[e], 4, to_y)

    def add(a, b):
        return (a.astype(F32) + b.astype(F32)).astype(BF16)

    def add_core(a, e):
        sums_core(a, e).wait_recv()
        PART[a, e, c] = add(PART[a, e, c], SIB[a, e])
        if a == 0:
            sums_y0(e).start()
        else:
            sums_on_right(e).start()
            sums_on_left(e).start()

    def add_second(a, e):
        if a == 0:
            sums_y0(e).wait_recv()
            PART[0, e, c, y] = add(PART[0, e, c, y], RY0[e])
            for k in range(1, NX):
                sums_x0(e, k).start()
        else:
            sums_on_right(e).wait_recv()
            PART[1, e, c, y, right(1)] = add(PART[1, e, c, y, right(1)], RX1[e, 1, 0])
            sums_on_left(e).wait_recv()
            PART[1, e, c, 1 - y, left(1)] = add(PART[1, e, c, 1 - y, left(1)], RX1[e, 1, 1])
            for k in (1, 3):
                sums_x1(e, k).start()

    def add_third(a, e):
        if a == 0:
            total = PART[0, e, c, y, x].astype(F32)
            for k in range(1, NX):
                sums_x0(e, k).wait_recv()
                total = total + RX0[e, k - 1].astype(F32)
            FIN[0, e] = total.astype(BF16)
        else:
            total = PART[1, e, c, :, x].astype(F32)
            for k in (1, 3):
                sums_x1(e, k).wait_recv()
                total = total + RX1[e, k - 1].astype(F32)
            PART[1, e, c, :, x] = total.astype(BF16)
            sums_y1(e).start()

    def add_fourth(a, e):
        sums_y1(e).wait_recv()
        FIN[1, e] = add(PART[1, e, c, y, x], RY1[e])

    for load in loads[3:]:
        load.wait()
    def back(part, k):
        return remote(
            BACK.at[part, ex_to(k)], BACK_IN.at[part, ex], back_s.at[part, k], back_r.at[part, k], (dp, ex_to(k))
        )

    def send_back(a, part):
        flat = halves(FIN[:, 2 * part:2 * part + 2].reshape(SLOT_ROWS // PARTS, D))
        rows = [
            dot(place(SLOT_ROWS // PARTS, SLOT_ROWS, message_of_blocks, part, j, True), flat[j]) for j in range(2)
        ]
        BACK[part] = (rows[0] + rows[1]).astype(BF16).reshape(GROUPS, ROWS, D // 2)
        for k in range(1, GROUPS):
            back(part, k).start()
        BACK_IN[part, ex] = BACK[part, ex]

    steps = {
        "A": arrive, "G": lambda a, e: gather_first(a, e, start), "S": second, "O": second_on, "T": third,
        "X": expert, "C": add_core, "D": add_second, "E": add_third, "F": add_fourth, "B": send_back,
    }
    for line in ORDER:
        for word in line.split():
            steps[word[0]](int(word[1]), int(word[2]))

    def grads(e, carry):
        weight_grads(e)
        return carry

    lax.fori_loop(0, LOCAL, grads, 0)
    for part in range(PARTS):
        for k in range(1, GROUPS):
            back(part, k).wait_recv()
    for j in range(2):
        rows = [
            dot(place(SLOT_ROWS, SLOT_ROWS, slots_of_message, part, j, True), BACK_IN[part].reshape(SLOT_ROWS, D // 2))
            for part in range(PARTS)
        ]
        SUMS[:, :, :, j * (D // 2):(j + 1) * (D // 2)] = (
            (rows[0] + rows[1]).astype(BF16).reshape(2, IMGS, SLOTS, D // 2)
        )

    param = jnp.zeros((SLOTS, D), F32)
    logit_grads = []
    for i in range(IMGS):
        dispatch, combine = DI[i], CO[i]
        combine_grad = dot(SUMS[0, i], G[i], 1, 1)
        dispatch_grad = dot(SUMS[1, i], T[i], 1, 1)
        combine_term = combine * (combine_grad - jnp.sum(combine * combine_grad, axis=0, keepdims=True))
        dispatch_term = dispatch * (dispatch_grad - jnp.sum(dispatch * dispatch_grad, axis=1, keepdims=True))
        logit_grad = (combine_term + dispatch_term).astype(BF16)
        logit_grads.append(logit_grad)
        param = param + dot(logit_grad, T[i])

    for j in range(GROUPS * SHARE):
        tile = slice(8 * (j % SHARE), 8 * (j % SHARE) + 8)
        PP[j // SHARE, tile] = param[8 * (j // 10):8 * (j // 10) + 8, 128 * (j % 10):128 * (j % 10) + 128]

    def ar_scatter(k):
        other, device = to_member(k)
        return remote(PP.at[other], AR1.at[k - 1], ar_s.at[k], ar_r.at[k], device)

    def ar_plane(k):
        return remote(AR2.at[plane], AR2.at[plane], mid_s.at[k], mid_r.at[k], to_plane(k))

    def ar_gather(k):
        return remote(GP.at[member], GP.at[member], last_s.at[k], last_r.at[k], to_member(k)[1])

    for k in range(1, GROUPS):
        ar_scatter(k).start()

    for i in range(IMGS):
        both = jnp.concatenate([DI[i].astype(BF16), logit_grads[i]], axis=0)
        rows = jnp.concatenate([SUMS[1, i], SP[...]], axis=0)
        grad_tokens[i] = dot(both.T, rows).astype(BF16)

    total = PP[member]
    for k in range(1, GROUPS):
        ar_scatter(k).wait_recv()
        total = total + AR1[k - 1]
    AR2[plane, :8 * SHARE] = total.astype(BF16)
    AR2[plane, 8 * SHARE:] = jnp.zeros((8, 128), BF16)
    for k in range(1, NX * NY * NH):
        ar_plane(k).start()
    for k in range(1, NX * NY * NH):
        ar_plane(k).wait_recv()
    total = AR2[0, :8 * SHARE].astype(F32)
    for k in range(1, NX * NY * NH):
        total = total + AR2[k, :8 * SHARE].astype(F32)
    GP[member] = total
    for k in range(1, GROUPS):
        ar_gather(k).start()

    def drain(e, carry):
        for a in range(2):
            gather_first(a, e, wait_send)
            gather_third(a, e).wait_send()
            sums_core(a, e).wait_send()
        gather_on_right(e, wait_send)
        gather_on_left(e, wait_send)
        for k in range(1, NX):
            gather_second_y(e, wait_send, k)
            sums_x0(e, k).wait_send()
        for k in (1, 3):
            gather_second_x(e, wait_send, k)
            sums_x1(e, k).wait_send()
        sums_on_right(e).wait_send()
        sums_on_left(e).wait_send()
        sums_y0(e).wait_send()
        sums_y1(e).wait_send()
        return carry

    lax.fori_loop(0, LOCAL, drain, 0)
    for k in range(1, GROUPS):
        for part in range(PARTS):
            a2a(part, k).wait_send()
            back(part, k).wait_send()
        ar_scatter(k).wait_send()
    for k in range(1, NX * NY * NH):
        ar_plane(k).wait_send()
    for k in range(1, GROUPS):
        ar_gather(k).wait_recv()
    for k in range(1, GROUPS):
        ar_gather(k).wait_send()
    for j in range(GROUPS * SHARE):
        tile = slice(8 * (j % SHARE), 8 * (j % SHARE) + 8)
        grad_param[8 * (j // 10):8 * (j // 10) + 8, 128 * (j % 10):128 * (j % 10) + 128] = GP[j // SHARE, tile]


def write_out(*refs):
    copies = [pltpu.make_async_copy(refs[i], refs[4 + i], refs[8].at[i]) for i in range(4)]
    for copy in copies:
        copy.start()
    for copy in copies:
        copy.wait()


def on_device(tokens, slot_param, inner_weight, outer_weight, output_grad):
    vmem = pl.BlockSpec(memory_space=pltpu.VMEM)
    chunk = (8 * SHARE, 128)
    dma = pltpu.SemaphoreType.DMA
    results = pl.pallas_call(
        kernel,
        out_shape=(
            pltpu.VMEM(tokens.shape, BF16),
            pltpu.VMEM(slot_param.shape, F32),
            pltpu.VMEM(inner_weight.shape, BF16),
            pltpu.VMEM(outer_weight.shape, BF16),
        ),
        in_specs=[pl.BlockSpec(memory_space=pltpu.HBM)] * 5,
        out_specs=(vmem,) * 4,
        scratch_shapes=[
            pltpu.VMEM((IMGS, PATCHES, D), BF16),
            pltpu.VMEM((IMGS, PATCHES, D), BF16),
            pltpu.VMEM((SLOTS, D), BF16),
            pltpu.VMEM((LOCAL, HIDDEN, D), BF16),
            pltpu.VMEM((LOCAL, HIDDEN, D), BF16),
            pltpu.VMEM((IMGS, SLOTS, PATCHES), F32),
            pltpu.VMEM((IMGS, SLOTS, PATCHES), F32),
            pltpu.VMEM((2 * IMGS, SLOTS, D), BF16),
            pltpu.VMEM((PARTS, GROUPS, ROWS, D // 2), BF16),
            pltpu.VMEM((PARTS, GROUPS, ROWS, D // 2), BF16),
            pltpu.VMEM((PARTS, GROUPS, ROWS, D // 2), BF16),
            pltpu.VMEM((PARTS, GROUPS, ROWS, D // 2), BF16),
            pltpu.VMEM((2, LOCAL, ROWS, D), BF16),
            pltpu.VMEM((2, IMGS, SLOTS, D), BF16),
            pltpu.VMEM((2, LOCAL, NC, NY, NX, ROWS, D), BF16),
            pltpu.VMEM((LOCAL, HIDDEN, BLOCKS * ROWS), BF16),
            pltpu.VMEM((LOCAL, HIDDEN, BLOCKS * ROWS), BF16),
            pltpu.VMEM((LOCAL, HIDDEN, BLOCKS * ROWS), F32),
            pltpu.VMEM((2, LOCAL, NC, NY, NX, ROWS, D), BF16),
            pltpu.VMEM((2, LOCAL, NY, NX, ROWS, D), BF16),
            pltpu.VMEM((LOCAL, NX, ROWS, D), BF16),
            pltpu.VMEM((LOCAL, NX - 1, ROWS, D), BF16),
            pltpu.VMEM((LOCAL, ROWS, D), BF16),
            pltpu.VMEM((LOCAL, NX - 1, NY, ROWS, D), BF16),
            pltpu.VMEM((GROUPS,) + chunk, F32),
            pltpu.VMEM((GROUPS - 1,) + chunk, F32),
            pltpu.VMEM((NX * NY * NH, 8 * SHARE + 8, 128), BF16),
            pltpu.VMEM((GROUPS,) + chunk, F32),
            dma((5,)), dma((PARTS, GROUPS)), dma((PARTS, GROUPS)), dma((PARTS, GROUPS)), dma((PARTS, GROUPS)),
            dma((2, LOCAL, 8)), dma((2, LOCAL, 8)), dma((2, LOCAL, 6)), dma((2, LOCAL, 6)),
            dma((GROUPS,)), dma((GROUPS,)), dma((NX * NY * NH,)), dma((NX * NY * NH,)),
            dma((GROUPS,)), dma((GROUPS,)),
        ],
        compiler_params=pltpu.CompilerParams(
            collective_id=0, has_side_effects=True, vmem_limit_bytes=54 * 2**20
        ),
    )(tokens, slot_param, inner_weight, outer_weight, output_grad)
    return pl.pallas_call(
        write_out,
        out_shape=tuple(jax.ShapeDtypeStruct(result.shape, result.dtype) for result in results),
        in_specs=[vmem] * 4,
        out_specs=(pl.BlockSpec(memory_space=pltpu.HBM),) * 4,
        scratch_shapes=[dma((4,))],
        compiler_params=pltpu.CompilerParams(vmem_limit_bytes=2**20),
    )(*[pltpu.with_memory_space_constraint(result, pltpu.VMEM) for result in results])


def solution(mesh):
    in_specs = (
        P(("dp", "expert"), None, None),
        P(),
        P("expert", "dp", None),
        P("expert", "dp", None),
        P(("dp", "expert"), None, None),
    )
    out_specs = (
        P(("dp", "expert"), None, None),
        P(),
        P("expert", "dp", None),
        P("expert", "dp", None),
    )
    return jax.shard_map(
        on_device, mesh=mesh, in_specs=in_specs, out_specs=out_specs, check_vma=False
    )
```

```python
import functools

import jax
import jax.numpy as jnp
from jax import lax
from jax.experimental import pallas as pl
from jax.experimental.pallas import tpu as pltpu
from jax.sharding import PartitionSpec as P

MESH = pl.DeviceIdType.MESH
F32 = jnp.float32
BF16 = jnp.bfloat16
NX, NY, NC = 4, 2, 2
NH, NZ = 2, 4
GROUPS = NH * NZ
LOCAL = 4
IMGS = 2
SLOTS = GROUPS * LOCAL
ROWS = 16
BLOCKS = NC * NY * NX
D = 1280
PATCHES = 256
HIDDEN = 320
TILE = 256
STEPS = D // TILE
PARTS = 2
SLOT_ROWS = 2 * IMGS * SLOTS
SHARE = SLOTS * D // (8 * 128 * GROUPS)

ORDER = (
    "A00 G01 G00 G10",
    "G11 A01 G12 G02",
    "S01 S10 G13 S00",
    "S11 G03 T01 O10",
    "S02 S12 X01 O11",
    "T00 S13 C01 T10",
    "X00 O12 T11 S03",
    "X10 T02 O13 C00",
    "X11 C10 T12 X02",
    "C11 D01 X12 C02",
    "T03 D10 T13 C12",
    "X03 D11 X13 C13",
    "D00 C03 D12 D13",
    "E11 D02 E10 E12",
    "E01 D03 F10 E00",
    "E13 F12 F11 B00",
    "E02 F13 E03 B01",
)


def dot(a, b, ca=1, cb=0):
    return lax.dot_general(a, b, (((ca,), (cb,)), ((), ())), preferred_element_type=F32)


def place(rows, columns, source_of, part, half, transposed=False):
    shape = (columns, rows) if transposed else (rows, columns)
    row = lax.broadcasted_iota(jnp.int32, shape, 1 if transposed else 0)
    column = lax.broadcasted_iota(jnp.int32, shape, 0 if transposed else 1)
    source, in_half = source_of(row, part, half)
    return jnp.where(jnp.logical_and(column == source, in_half), 1.0, 0.0).astype(BF16)


def slots_of_message(r, part, half):
    group, array, expert, image = r // 16, (r // 4) % 2, (r // 2) % 2, r % 2
    return array * 64 + image * 32 + group * 4 + 2 * part + expert, (r // 8) % 2 == half


def message_of_blocks(r, part, half):
    array, expert, group, image = r // 32, (r // 16) % 2, (r // 2) % 8, r % 2
    return group * 16 + half * 8 + array * 4 + expert * 2 + image, r >= 0


def halves(array):
    return array[:, : D // 2], array[:, D // 2 :]


def kernel(
    tokens, slot_param, inner, outer, cotangent,
    grad_tokens, grad_param, grad_inner, grad_outer,
    T, G, SP, WI, WO, DI, CO, X, MSG, MSG_IN, BACK, BACK_IN, FIN, SUMS, BY_BLOCK, BY_MESSAGE, BY_SLOT,
    R, ACT, SCA, SLOPE, PART, SIB, RY0, RX0, RY1, RX1,
    PP, AR1, AR2, GP,
    in_sem, a2a_s, a2a_r, back_s, back_r, ag_s, ag_r, rs_s, rs_r, ar_s, ar_r, mid_s, mid_r, last_s, last_r,
):
    dp, ex = lax.axis_index("dp"), lax.axis_index("expert")
    x, y, c = dp // 4, (dp // 2) % 2, dp % 2
    h, z = ex // NZ, ex % NZ

    def at_dp(px, py, pc):
        return (px * 4 + py * 2 + pc, ex)

    def right(k):
        return (x + k) % NX

    def left(k):
        return (x + NX - k) % NX

    def to_x(k):
        return at_dp(right(k), y, c)

    to_y = at_dp(x, 1 - y, c)
    to_core = at_dp(x, y, 1 - c)

    def ex_to(k):
        return (ex + k) % GROUPS

    def ex_from(k):
        return (ex + GROUPS - k) % GROUPS

    def remote(src, dst, send, recv, device):
        return pltpu.make_async_remote_copy(
            src_ref=src, dst_ref=dst, send_sem=send, recv_sem=recv, device_id=device, device_id_type=MESH
        )

    member = c * NZ + z
    plane = (x * NY + y) * NH + h

    def to_member(k):
        other = (member + k) % GROUPS
        return other, ((x * NY + y) * NC + other // NZ, h * NZ + other % NZ)

    def to_plane(k):
        other = (plane + k) % (NX * NY * NH)
        return (other // NH * NC + c, other % NH * NZ + z)

    barrier = pltpu.get_barrier_semaphore()
    partners = [
        (at_dp(right(dx), (y + dy) % NY, c)[0], (h + dh) % NH * NZ + z)
        for dx in (2, 1, 3, 0) for dh in (1, 0) for dy in (1, 0) if dx or dy
    ]
    partners += [(dp, ex_to(k)) for k in range(GROUPS - 1, 0, -1)]
    partners += [(at_dp(x, y, 1 - c)[0], h * NZ + (z + k) % NZ) for k in range(1, NZ)] + [to_core]
    for partner in partners:
        pl.semaphore_signal(barrier, inc=1, device_id=partner, device_id_type=MESH)

    loads = [
        pltpu.make_async_copy(slot_param, SP, in_sem.at[0]),
        pltpu.make_async_copy(tokens, T, in_sem.at[1]),
        pltpu.make_async_copy(cotangent, G, in_sem.at[2]),
        pltpu.make_async_copy(inner, WI, in_sem.at[3]),
        pltpu.make_async_copy(outer, WO, in_sem.at[4]),
    ]
    for load in loads:
        load.start()
    for load in loads[:3]:
        load.wait()

    for i in range(IMGS):
        logits = dot(SP[...], T[i], 1, 1)
        ed = jnp.exp(logits - jnp.max(logits, axis=1, keepdims=True))
        dispatch = ed / jnp.sum(ed, axis=1, keepdims=True)
        ec = jnp.exp(logits - jnp.max(logits, axis=0, keepdims=True))
        combine = ec / jnp.sum(ec, axis=0, keepdims=True)
        DI[i] = dispatch
        CO[i] = combine
        X[i] = dot(dispatch.astype(BF16), T[i]).astype(BF16)
        X[IMGS + i] = dot(combine.astype(BF16), G[i]).astype(BF16)
    for j in range(2):
        BY_BLOCK[j] = place(SLOT_ROWS // PARTS, SLOT_ROWS, message_of_blocks, 0, j)
        BY_MESSAGE[j] = place(SLOT_ROWS // PARTS, SLOT_ROWS, message_of_blocks, 0, j, True)
        for part in range(PARTS):
            BY_SLOT[part, j] = place(SLOT_ROWS, SLOT_ROWS, slots_of_message, part, j, True)
    flat = halves(X[...].reshape(SLOT_ROWS, D))
    for part in range(PARTS):
        rows = [dot(place(SLOT_ROWS, SLOT_ROWS, slots_of_message, part, j), flat[j]) for j in range(2)]
        MSG[part] = (rows[0] + rows[1]).astype(BF16).reshape(GROUPS, ROWS, D // 2)

    pl.semaphore_wait(barrier, len(partners))

    def a2a(part, k):
        return remote(
            MSG.at[part, ex_to(k)], MSG_IN.at[part, ex], a2a_s.at[part, k], a2a_r.at[part, k], (dp, ex_to(k))
        )

    for part in range(PARTS):
        for k in range(1, GROUPS):
            a2a(part, k).start()
    for part in range(PARTS):
        MSG_IN[part, ex] = MSG[part, ex]

    def arrive(a, part):
        for k in range(1, GROUPS):
            a2a(part, k).wait_recv()
        flat = MSG_IN[part].reshape(SLOT_ROWS, D // 2)
        for j in range(2):
            rows = dot(BY_BLOCK[j], flat).astype(BF16)
            rows = rows.reshape(2, LOCAL // PARTS, ROWS, D // 2)
            for a in range(2):
                for e in range(LOCAL // PARTS):
                    R[a, 2 * part + e, c, y, x, :, j * (D // 2):(j + 1) * (D // 2)] = rows[a, e]

    def block_copy(a, e, py, px, sem, device):
        ref = R.at[a, e, c, py, px]
        return remote(ref, ref, ag_s.at[a, e, sem], ag_r.at[a, e, sem], device)

    def gather_first(a, e, act):
        if a == 1:
            act(block_copy(1, e, y, x, 3, to_y))
        for k in range(1, NX) if a == 0 else (1, 3):
            act(block_copy(a, e, y, x, k - 1, to_x(k)))
        if a == 0:
            act(block_copy(0, e, y, x, 3, to_y))

    def gather_second_x(e, act, k):
        act(block_copy(1, e, 1 - y, x, 3 + k, to_x(k)))

    def gather_second_y(e, act, k):
        act(block_copy(0, e, y, left(k), 3 + k, to_y))

    def gather_on_right(e, act):
        act(block_copy(1, e, y, left(1), 1, to_x(1)))

    def gather_on_left(e, act):
        act(block_copy(1, e, 1 - y, right(1), 5, to_x(3)))

    def gather_third(a, e):
        ref = R.at[a, e, c]
        return remote(ref, ref, ag_s.at[a, e, 7], ag_r.at[a, e, 7], to_core)

    def start(copy):
        copy.start()

    def wait_send(copy):
        copy.wait_send()

    def wait_recv(a, e, sem):
        block_copy(a, e, y, x, sem, to_y).wait_recv()

    def second(a, e):
        if a == 0:
            for k in (1, 3, 2):
                wait_recv(0, e, k - 1)
                gather_second_y(e, start, k)
        else:
            wait_recv(1, e, 3)
            for k in (1, 3):
                gather_second_x(e, start, k)
            wait_recv(1, e, 0)
            gather_on_right(e, start)

    def second_on(a, e):
        wait_recv(1, e, 6)
        gather_on_left(e, start)

    def third(a, e):
        for sem in (3, 4, 5, 6) if a == 0 else (2, 1, 4, 5):
            wait_recv(a, e, sem)
        gather_third(a, e).start()

    def expert(a, e):
        gather_third(a, e).wait_recv()
        rows = R[a, e].reshape(BLOCKS * ROWS, D)
        if a == 0:
            hidden = dot(WI[e], rows, 1, 1)
            phi = 0.5 * (1.0 + lax.erf(hidden * 0.7071067811865476))
            SLOPE[e] = phi + hidden * jnp.exp(-0.5 * hidden * hidden) * 0.3989422804014327
            act, kept, weight = (hidden * phi).astype(BF16), ACT, WO
        else:
            act, kept, weight = (dot(WO[e], rows, 1, 1) * SLOPE[e]).astype(BF16), SCA, WI
        kept[e] = act
        act_t = act.T
        for n in range(STEPS):
            cols = slice(n * TILE, (n + 1) * TILE)
            PART[a, e, :, :, :, :, cols] = (
                dot(act_t, weight[e, :, cols]).astype(BF16).reshape(NC, NY, NX, ROWS, TILE)
            )
        sums_core(a, e).start()

    def weight_grads(e):
        for n in range(STEPS):
            cols = slice(n * TILE, (n + 1) * TILE)
            rows_in = R[0, e, :, :, :, :, cols].reshape(BLOCKS * ROWS, TILE)
            rows_grad = R[1, e, :, :, :, :, cols].reshape(BLOCKS * ROWS, TILE)
            grad_outer[e, :, cols] = dot(ACT[e], rows_grad).astype(BF16)
            grad_inner[e, :, cols] = dot(SCA[e], rows_in).astype(BF16)

    def sum_copy(a, e, src, dst, sem, device):
        return remote(src, dst, rs_s.at[a, e, sem], rs_r.at[a, e, sem], device)

    def sums_core(a, e):
        return sum_copy(a, e, PART.at[a, e, 1 - c], SIB.at[a, e], 0, to_core)

    def sums_y0(e):
        return sum_copy(0, e, PART.at[0, e, c, 1 - y], RY0.at[e], 4, to_y)

    def sums_x0(e, k):
        return sum_copy(0, e, PART.at[0, e, c, y, right(k)], RX0.at[e, k - 1], k, to_x(k))

    def sums_x1(e, k):
        return sum_copy(1, e, PART.at[1, e, c, :, right(k)], RX1.at[e, k - 1], k, to_x(k))

    def sums_on_right(e):
        return sum_copy(1, e, PART.at[1, e, c, y, right(2)], RX1.at[e, 1, 0], 2, to_x(1))

    def sums_on_left(e):
        return sum_copy(1, e, PART.at[1, e, c, 1 - y, right(2)], RX1.at[e, 1, 1], 5, to_x(3))

    def sums_y1(e):
        return sum_copy(1, e, PART.at[1, e, c, 1 - y, x], RY1.at[e], 4, to_y)

    def add(a, b):
        return (a.astype(F32) + b.astype(F32)).astype(BF16)

    def add_core(a, e):
        sums_core(a, e).wait_recv()
        PART[a, e, c] = add(PART[a, e, c], SIB[a, e])
        if a == 0:
            sums_y0(e).start()
        else:
            sums_on_right(e).start()
            sums_on_left(e).start()

    def add_second(a, e):
        if a == 0:
            sums_y0(e).wait_recv()
            PART[0, e, c, y] = add(PART[0, e, c, y], RY0[e])
            for k in range(1, NX):
                sums_x0(e, k).start()
        else:
            sums_on_right(e).wait_recv()
            PART[1, e, c, y, right(1)] = add(PART[1, e, c, y, right(1)], RX1[e, 1, 0])
            sums_on_left(e).wait_recv()
            PART[1, e, c, 1 - y, left(1)] = add(PART[1, e, c, 1 - y, left(1)], RX1[e, 1, 1])
            for k in (1, 3):
                sums_x1(e, k).start()

    def add_third(a, e):
        if a == 0:
            total = PART[0, e, c, y, x].astype(F32)
            for k in range(1, NX):
                sums_x0(e, k).wait_recv()
                total = total + RX0[e, k - 1].astype(F32)
            FIN[0, e] = total.astype(BF16)
        else:
            total = PART[1, e, c, :, x].astype(F32)
            for k in (1, 3):
                sums_x1(e, k).wait_recv()
                total = total + RX1[e, k - 1].astype(F32)
            PART[1, e, c, :, x] = total.astype(BF16)
            sums_y1(e).start()

    def add_fourth(a, e):
        sums_y1(e).wait_recv()
        FIN[1, e] = add(PART[1, e, c, y, x], RY1[e])

    for load in loads[3:]:
        load.wait()
    def back(part, k):
        return remote(
            BACK.at[part, ex_to(k)], BACK_IN.at[part, ex], back_s.at[part, k], back_r.at[part, k], (dp, ex_to(k))
        )

    def send_back(a, part):
        flat = halves(FIN[:, 2 * part:2 * part + 2].reshape(SLOT_ROWS // PARTS, D))
        rows = [dot(BY_MESSAGE[j], flat[j]) for j in range(2)]
        BACK[part] = (rows[0] + rows[1]).astype(BF16).reshape(GROUPS, ROWS, D // 2)
        for k in range(1, GROUPS):
            back(part, k).start()
        BACK_IN[part, ex] = BACK[part, ex]

    steps = {
        "A": arrive, "G": lambda a, e: gather_first(a, e, start), "S": second, "O": second_on, "T": third,
        "X": expert, "C": add_core, "D": add_second, "E": add_third, "F": add_fourth, "B": send_back,
    }
    for line in ORDER:
        for word in line.split():
            steps[word[0]](int(word[1]), int(word[2]))

    def grads(e, carry):
        weight_grads(e)
        return carry

    lax.fori_loop(0, LOCAL, grads, 0)
    for k in range(1, GROUPS):
        back(0, k).wait_recv()
    first = [dot(BY_SLOT[0, j], BACK_IN[0].reshape(SLOT_ROWS, D // 2)) for j in range(2)]
    for k in range(1, GROUPS):
        back(1, k).wait_recv()
    for j in range(2):
        rows = first[j] + dot(BY_SLOT[1, j], BACK_IN[1].reshape(SLOT_ROWS, D // 2))
        SUMS[:, :, :, j * (D // 2):(j + 1) * (D // 2)] = rows.astype(BF16).reshape(2, IMGS, SLOTS, D // 2)

    param = jnp.zeros((SLOTS, D), F32)
    logit_grads = []
    for i in range(IMGS):
        dispatch, combine = DI[i], CO[i]
        combine_grad = dot(SUMS[0, i], G[i], 1, 1)
        dispatch_grad = dot(SUMS[1, i], T[i], 1, 1)
        combine_term = combine * (combine_grad - jnp.sum(combine * combine_grad, axis=0, keepdims=True))
        dispatch_term = dispatch * (dispatch_grad - jnp.sum(dispatch * dispatch_grad, axis=1, keepdims=True))
        logit_grad = (combine_term + dispatch_term).astype(BF16)
        logit_grads.append(logit_grad)
        param = param + dot(logit_grad, T[i])

    for j in range(GROUPS * SHARE):
        tile = slice(8 * (j % SHARE), 8 * (j % SHARE) + 8)
        PP[j // SHARE, tile] = param[8 * (j // 10):8 * (j // 10) + 8, 128 * (j % 10):128 * (j % 10) + 128]

    def ar_scatter(k):
        other, device = to_member(k)
        return remote(PP.at[other], AR1.at[k - 1], ar_s.at[k], ar_r.at[k], device)

    def ar_plane(k):
        return remote(AR2.at[plane], AR2.at[plane], mid_s.at[k], mid_r.at[k], to_plane(k))

    def ar_gather(k):
        return remote(GP.at[member], GP.at[member], last_s.at[k], last_r.at[k], to_member(k)[1])

    for k in range(1, GROUPS):
        ar_scatter(k).start()

    for i in range(IMGS):
        both = jnp.concatenate([DI[i].astype(BF16), logit_grads[i]], axis=0)
        rows = jnp.concatenate([SUMS[1, i], SP[...]], axis=0)
        grad_tokens[i] = dot(both.T, rows).astype(BF16)

    total = PP[member]
    for k in range(1, GROUPS):
        ar_scatter(k).wait_recv()
        total = total + AR1[k - 1]
    AR2[plane, :8 * SHARE] = total.astype(BF16)
    AR2[plane, 8 * SHARE:] = jnp.zeros((8, 128), BF16)
    for k in range(1, NX * NY * NH):
        ar_plane(k).start()
    for k in range(1, NX * NY * NH):
        ar_plane(k).wait_recv()
    total = AR2[0, :8 * SHARE].astype(F32)
    for k in range(1, NX * NY * NH):
        total = total + AR2[k, :8 * SHARE].astype(F32)
    GP[member] = total
    for k in range(1, GROUPS):
        ar_gather(k).start()

    def drain(e, carry):
        for a in range(2):
            gather_first(a, e, wait_send)
            gather_third(a, e).wait_send()
            sums_core(a, e).wait_send()
        gather_on_right(e, wait_send)
        gather_on_left(e, wait_send)
        for k in range(1, NX):
            gather_second_y(e, wait_send, k)
            sums_x0(e, k).wait_send()
        for k in (1, 3):
            gather_second_x(e, wait_send, k)
            sums_x1(e, k).wait_send()
        sums_on_right(e).wait_send()
        sums_on_left(e).wait_send()
        sums_y0(e).wait_send()
        sums_y1(e).wait_send()
        return carry

    lax.fori_loop(0, LOCAL, drain, 0)
    for k in range(1, GROUPS):
        for part in range(PARTS):
            a2a(part, k).wait_send()
            back(part, k).wait_send()
        ar_scatter(k).wait_send()
    for k in range(1, NX * NY * NH):
        ar_plane(k).wait_send()
    for k in range(1, GROUPS):
        ar_gather(k).wait_recv()
    for k in range(1, GROUPS):
        ar_gather(k).wait_send()
    for j in range(GROUPS * SHARE):
        tile = slice(8 * (j % SHARE), 8 * (j % SHARE) + 8)
        grad_param[8 * (j // 10):8 * (j // 10) + 8, 128 * (j % 10):128 * (j % 10) + 128] = GP[j // SHARE, tile]


def write_out(*refs):
    pairs = [(refs[1], refs[5])]
    for i in (0, 2, 3):
        pairs += [(refs[i].at[j], refs[4 + i].at[j]) for j in range(refs[i].shape[0])]
    copies = [pltpu.make_async_copy(*pair, refs[8].at[i]) for i, pair in enumerate(pairs)]
    for copy in copies:
        copy.start()
    for copy in copies:
        copy.wait()


def on_device(tokens, slot_param, inner_weight, outer_weight, output_grad):
    vmem = pl.BlockSpec(memory_space=pltpu.VMEM)
    chunk = (8 * SHARE, 128)
    dma = pltpu.SemaphoreType.DMA
    results = pl.pallas_call(
        kernel,
        out_shape=(
            pltpu.VMEM(tokens.shape, BF16),
            pltpu.VMEM(slot_param.shape, F32),
            pltpu.VMEM(inner_weight.shape, BF16),
            pltpu.VMEM(outer_weight.shape, BF16),
        ),
        in_specs=[pl.BlockSpec(memory_space=pltpu.HBM)] * 5,
        out_specs=(vmem,) * 4,
        scratch_shapes=[
            pltpu.VMEM((IMGS, PATCHES, D), BF16),
            pltpu.VMEM((IMGS, PATCHES, D), BF16),
            pltpu.VMEM((SLOTS, D), BF16),
            pltpu.VMEM((LOCAL, HIDDEN, D), BF16),
            pltpu.VMEM((LOCAL, HIDDEN, D), BF16),
            pltpu.VMEM((IMGS, SLOTS, PATCHES), F32),
            pltpu.VMEM((IMGS, SLOTS, PATCHES), F32),
            pltpu.VMEM((2 * IMGS, SLOTS, D), BF16),
            pltpu.VMEM((PARTS, GROUPS, ROWS, D // 2), BF16),
            pltpu.VMEM((PARTS, GROUPS, ROWS, D // 2), BF16),
            pltpu.VMEM((PARTS, GROUPS, ROWS, D // 2), BF16),
            pltpu.VMEM((PARTS, GROUPS, ROWS, D // 2), BF16),
            pltpu.VMEM((2, LOCAL, ROWS, D), BF16),
            pltpu.VMEM((2, IMGS, SLOTS, D), BF16),
            pltpu.VMEM((2, SLOT_ROWS // PARTS, SLOT_ROWS), BF16),
            pltpu.VMEM((2, SLOT_ROWS, SLOT_ROWS // PARTS), BF16),
            pltpu.VMEM((PARTS, 2, SLOT_ROWS, SLOT_ROWS), BF16),
            pltpu.VMEM((2, LOCAL, NC, NY, NX, ROWS, D), BF16),
            pltpu.VMEM((LOCAL, HIDDEN, BLOCKS * ROWS), BF16),
            pltpu.VMEM((LOCAL, HIDDEN, BLOCKS * ROWS), BF16),
            pltpu.VMEM((LOCAL, HIDDEN, BLOCKS * ROWS), F32),
            pltpu.VMEM((2, LOCAL, NC, NY, NX, ROWS, D), BF16),
            pltpu.VMEM((2, LOCAL, NY, NX, ROWS, D), BF16),
            pltpu.VMEM((LOCAL, NX, ROWS, D), BF16),
            pltpu.VMEM((LOCAL, NX - 1, ROWS, D), BF16),
            pltpu.VMEM((LOCAL, ROWS, D), BF16),
            pltpu.VMEM((LOCAL, NX - 1, NY, ROWS, D), BF16),
            pltpu.VMEM((GROUPS,) + chunk, F32),
            pltpu.VMEM((GROUPS - 1,) + chunk, F32),
            pltpu.VMEM((NX * NY * NH, 8 * SHARE + 8, 128), BF16),
            pltpu.VMEM((GROUPS,) + chunk, F32),
            dma((5,)), dma((PARTS, GROUPS)), dma((PARTS, GROUPS)), dma((PARTS, GROUPS)), dma((PARTS, GROUPS)),
            dma((2, LOCAL, 8)), dma((2, LOCAL, 8)), dma((2, LOCAL, 6)), dma((2, LOCAL, 6)),
            dma((GROUPS,)), dma((GROUPS,)), dma((NX * NY * NH,)), dma((NX * NY * NH,)),
            dma((GROUPS,)), dma((GROUPS,)),
        ],
        compiler_params=pltpu.CompilerParams(
            collective_id=0, has_side_effects=True, vmem_limit_bytes=54 * 2**20
        ),
    )(tokens, slot_param, inner_weight, outer_weight, output_grad)
    return pl.pallas_call(
        write_out,
        out_shape=tuple(jax.ShapeDtypeStruct(result.shape, result.dtype) for result in results),
        in_specs=[vmem] * 4,
        out_specs=(pl.BlockSpec(memory_space=pltpu.HBM),) * 4,
        scratch_shapes=[dma((1 + IMGS + 2 * LOCAL,))],
        compiler_params=pltpu.CompilerParams(vmem_limit_bytes=2**20),
    )(*[pltpu.with_memory_space_constraint(result, pltpu.VMEM) for result in results])


def solution(mesh):
    in_specs = (
        P(("dp", "expert"), None, None),
        P(),
        P("expert", "dp", None),
        P("expert", "dp", None),
        P(("dp", "expert"), None, None),
    )
    out_specs = (
        P(("dp", "expert"), None, None),
        P(),
        P("expert", "dp", None),
        P("expert", "dp", None),
    )
    return jax.shard_map(
        on_device, mesh=mesh, in_specs=in_specs, out_specs=out_specs, check_vma=False
    )
```

```python
import functools

import jax
import jax.numpy as jnp
from jax import lax
from jax.experimental import pallas as pl
from jax.experimental.pallas import tpu as pltpu
from jax.sharding import PartitionSpec as P

MESH = pl.DeviceIdType.MESH
F32 = jnp.float32
BF16 = jnp.bfloat16
NX, NY, NC = 4, 2, 2
NH, NZ = 2, 4
GROUPS = NH * NZ
FAR_FIRST = (6, 5, 7, 2, 4, 1, 3)
PLANE_FAR_FIRST = (11, 9, 10, 7, 15, 8, 5, 13, 6, 14, 3, 1, 4, 12, 2)
LOCAL = 4
IMGS = 2
SLOTS = GROUPS * LOCAL
ROWS = 16
BLOCKS = NC * NY * NX
D = 1280
PATCHES = 256
HIDDEN = 320
TILE = 256
STEPS = D // TILE
PARTS = 2
SLOT_ROWS = 2 * IMGS * SLOTS
SHARE = SLOTS * D // (8 * 128 * GROUPS)

ORDER = (
    "A00 G01 G00 G10",
    "G11 A01 G12 G02",
    "S01 S10 G13 S00",
    "S11 G03 T01 O10",
    "S02 S12 X01 O11",
    "T00 S13 C01 T10",
    "X00 O12 T11 S03",
    "X10 T02 O13 C00",
    "X11 C10 T12 X02",
    "C11 D01 X12 C02",
    "T03 D10 T13 C12",
    "X03 D11 X13 C13",
    "D00 C03 D12 D13",
    "E11 D02 E10 E12",
    "E01 D03 F10 E00",
    "E13 F12 F11 B00",
    "E02 F13 E03 B01",
)


def dot(a, b, ca=1, cb=0):
    return lax.dot_general(a, b, (((ca,), (cb,)), ((), ())), preferred_element_type=F32)


def place(rows, columns, source_of, part, half, transposed=False):
    shape = (columns, rows) if transposed else (rows, columns)
    row = lax.broadcasted_iota(jnp.int32, shape, 1 if transposed else 0)
    column = lax.broadcasted_iota(jnp.int32, shape, 0 if transposed else 1)
    source, in_half = source_of(row, part, half)
    return jnp.where(jnp.logical_and(column == source, in_half), 1.0, 0.0).astype(BF16)


def slots_of_message(r, part, half):
    group, array, expert, image = r // 16, (r // 4) % 2, (r // 2) % 2, r % 2
    return array * 64 + image * 32 + group * 4 + 2 * part + expert, (r // 8) % 2 == half


def message_of_blocks(r, part, half):
    array, expert, group, image = r // 32, (r // 16) % 2, (r // 2) % 8, r % 2
    return group * 16 + half * 8 + array * 4 + expert * 2 + image, r >= 0


def halves(array):
    return array[:, : D // 2], array[:, D // 2 :]


def kernel(
    tokens, slot_param, inner, outer, cotangent,
    grad_tokens, grad_param, grad_inner, grad_outer,
    T, G, SP, WI, WO, DI, CO, X, MSG, MSG_IN, BACK, BACK_IN, FIN, SUMS, BY_BLOCK, BY_MESSAGE, BY_SLOT,
    R, ACT, SCA, SLOPE, PART, SIB, RY0, RX0, RY1, RX1,
    PP, AR1, AR2, GP,
    in_sem, a2a_s, a2a_r, back_s, back_r, ag_s, ag_r, rs_s, rs_r, ar_s, ar_r, mid_s, mid_r, last_s, last_r,
):
    dp, ex = lax.axis_index("dp"), lax.axis_index("expert")
    x, y, c = dp // 4, (dp // 2) % 2, dp % 2
    h, z = ex // NZ, ex % NZ

    def at_dp(px, py, pc):
        return (px * 4 + py * 2 + pc, ex)

    def right(k):
        return (x + k) % NX

    def left(k):
        return (x + NX - k) % NX

    def to_x(k):
        return at_dp(right(k), y, c)

    to_y = at_dp(x, 1 - y, c)
    to_core = at_dp(x, y, 1 - c)

    def ex_to(k):
        return (h + k // NZ) % NH * NZ + (z + k) % NZ

    def remote(src, dst, send, recv, device):
        return pltpu.make_async_remote_copy(
            src_ref=src, dst_ref=dst, send_sem=send, recv_sem=recv, device_id=device, device_id_type=MESH
        )

    member = c * NZ + z
    plane = (x * NY + y) * NH + h

    def to_member(k):
        core, depth = (c + k // NZ) % NC, (z + k) % NZ
        return core * NZ + depth, ((x * NY + y) * NC + core, h * NZ + depth)

    def to_plane(k):
        device = at_dp((x + k // 4) % NX, (y + k // 2) % NY, c)[0]
        return device, (h + k) % NH * NZ + z

    barrier = pltpu.get_barrier_semaphore()
    partners = [
        (at_dp(right(dx), (y + dy) % NY, c)[0], (h + dh) % NH * NZ + z)
        for dx in (2, 1, 3, 0) for dh in (1, 0) for dy in (1, 0) if dx or dy
    ]
    partners += [(dp, ex_to(k)) for k in range(GROUPS - 1, 0, -1)]
    partners += [(at_dp(x, y, 1 - c)[0], h * NZ + (z + k) % NZ) for k in range(1, NZ)] + [to_core]
    for partner in partners:
        pl.semaphore_signal(barrier, inc=1, device_id=partner, device_id_type=MESH)

    loads = [
        pltpu.make_async_copy(slot_param, SP, in_sem.at[0]),
        pltpu.make_async_copy(tokens, T, in_sem.at[1]),
        pltpu.make_async_copy(cotangent, G, in_sem.at[2]),
        pltpu.make_async_copy(inner, WI, in_sem.at[3]),
        pltpu.make_async_copy(outer, WO, in_sem.at[4]),
    ]
    for load in loads:
        load.start()
    for load in loads[:3]:
        load.wait()

    for i in range(IMGS):
        logits = dot(SP[...], T[i], 1, 1)
        ed = jnp.exp(logits - jnp.max(logits, axis=1, keepdims=True))
        dispatch = ed / jnp.sum(ed, axis=1, keepdims=True)
        ec = jnp.exp(logits - jnp.max(logits, axis=0, keepdims=True))
        combine = ec / jnp.sum(ec, axis=0, keepdims=True)
        DI[i] = dispatch
        CO[i] = combine
        X[i] = dot(dispatch.astype(BF16), T[i]).astype(BF16)
        X[IMGS + i] = dot(combine.astype(BF16), G[i]).astype(BF16)
    for j in range(2):
        BY_BLOCK[j] = place(SLOT_ROWS // PARTS, SLOT_ROWS, message_of_blocks, 0, j)
        BY_MESSAGE[j] = place(SLOT_ROWS // PARTS, SLOT_ROWS, message_of_blocks, 0, j, True)
        for part in range(PARTS):
            BY_SLOT[part, j] = place(SLOT_ROWS, SLOT_ROWS, slots_of_message, part, j, True)
    flat = halves(X[...].reshape(SLOT_ROWS, D))
    for part in range(PARTS):
        rows = [dot(place(SLOT_ROWS, SLOT_ROWS, slots_of_message, part, j), flat[j]) for j in range(2)]
        MSG[part] = (rows[0] + rows[1]).astype(BF16).reshape(GROUPS, ROWS, D // 2)

    pl.semaphore_wait(barrier, len(partners))

    def a2a(part, k):
        return remote(
            MSG.at[part, ex_to(k)], MSG_IN.at[part, ex], a2a_s.at[part, k], a2a_r.at[part, k], (dp, ex_to(k))
        )

    for part in range(PARTS):
        for k in FAR_FIRST:
            a2a(part, k).start()
    for part in range(PARTS):
        MSG_IN[part, ex] = MSG[part, ex]

    def arrive(a, part):
        for k in range(1, GROUPS):
            a2a(part, k).wait_recv()
        flat = MSG_IN[part].reshape(SLOT_ROWS, D // 2)
        for j in range(2):
            rows = dot(BY_BLOCK[j], flat).astype(BF16)
            rows = rows.reshape(2, LOCAL // PARTS, ROWS, D // 2)
            for a in range(2):
                for e in range(LOCAL // PARTS):
                    R[a, 2 * part + e, c, y, x, :, j * (D // 2):(j + 1) * (D // 2)] = rows[a, e]

    def block_copy(a, e, py, px, sem, device):
        ref = R.at[a, e, c, py, px]
        return remote(ref, ref, ag_s.at[a, e, sem], ag_r.at[a, e, sem], device)

    def gather_first(a, e, act):
        if a == 1:
            act(block_copy(1, e, y, x, 3, to_y))
        for k in range(1, NX) if a == 0 else (1, 3):
            act(block_copy(a, e, y, x, k - 1, to_x(k)))
        if a == 0:
            act(block_copy(0, e, y, x, 3, to_y))

    def gather_second_x(e, act, k):
        act(block_copy(1, e, 1 - y, x, 3 + k, to_x(k)))

    def gather_second_y(e, act, k):
        act(block_copy(0, e, y, left(k), 3 + k, to_y))

    def gather_on_right(e, act):
        act(block_copy(1, e, y, left(1), 1, to_x(1)))

    def gather_on_left(e, act):
        act(block_copy(1, e, 1 - y, right(1), 5, to_x(3)))

    def gather_third(a, e):
        ref = R.at[a, e, c]
        return remote(ref, ref, ag_s.at[a, e, 7], ag_r.at[a, e, 7], to_core)

    def start(copy):
        copy.start()

    def wait_send(copy):
        copy.wait_send()

    def wait_recv(a, e, sem):
        block_copy(a, e, y, x, sem, to_y).wait_recv()

    def second(a, e):
        if a == 0:
            for k in (1, 3, 2):
                wait_recv(0, e, k - 1)
                gather_second_y(e, start, k)
        else:
            wait_recv(1, e, 3)
            for k in (1, 3):
                gather_second_x(e, start, k)
            wait_recv(1, e, 0)
            gather_on_right(e, start)

    def second_on(a, e):
        wait_recv(1, e, 6)
        gather_on_left(e, start)

    def third(a, e):
        for sem in (3, 4, 5, 6) if a == 0 else (2, 1, 4, 5):
            wait_recv(a, e, sem)
        gather_third(a, e).start()

    def expert(a, e):
        gather_third(a, e).wait_recv()
        rows = R[a, e].reshape(BLOCKS * ROWS, D)
        if a == 0:
            hidden = dot(WI[e], rows, 1, 1)
            phi = 0.5 * (1.0 + lax.erf(hidden * 0.7071067811865476))
            SLOPE[e] = phi + hidden * jnp.exp(-0.5 * hidden * hidden) * 0.3989422804014327
            act, kept, weight = (hidden * phi).astype(BF16), ACT, WO
        else:
            act, kept, weight = (dot(WO[e], rows, 1, 1) * SLOPE[e]).astype(BF16), SCA, WI
        kept[e] = act
        act_t = act.T
        for n in range(STEPS):
            cols = slice(n * TILE, (n + 1) * TILE)
            PART[a, e, :, :, :, :, cols] = (
                dot(act_t, weight[e, :, cols]).astype(BF16).reshape(NC, NY, NX, ROWS, TILE)
            )
        sums_core(a, e).start()

    def weight_grads(e):
        for n in range(STEPS):
            cols = slice(n * TILE, (n + 1) * TILE)
            rows_in = R[0, e, :, :, :, :, cols].reshape(BLOCKS * ROWS, TILE)
            rows_grad = R[1, e, :, :, :, :, cols].reshape(BLOCKS * ROWS, TILE)
            grad_outer[e, :, cols] = dot(ACT[e], rows_grad).astype(BF16)
            grad_inner[e, :, cols] = dot(SCA[e], rows_in).astype(BF16)

    def sum_copy(a, e, src, dst, sem, device):
        return remote(src, dst, rs_s.at[a, e, sem], rs_r.at[a, e, sem], device)

    def sums_core(a, e):
        return sum_copy(a, e, PART.at[a, e, 1 - c], SIB.at[a, e], 0, to_core)

    def sums_y0(e):
        return sum_copy(0, e, PART.at[0, e, c, 1 - y], RY0.at[e], 4, to_y)

    def sums_x0(e, k):
        return sum_copy(0, e, PART.at[0, e, c, y, right(k)], RX0.at[e, k - 1], k, to_x(k))

    def sums_x1(e, k):
        return sum_copy(1, e, PART.at[1, e, c, :, right(k)], RX1.at[e, k - 1], k, to_x(k))

    def sums_on_right(e):
        return sum_copy(1, e, PART.at[1, e, c, y, right(2)], RX1.at[e, 1, 0], 2, to_x(1))

    def sums_on_left(e):
        return sum_copy(1, e, PART.at[1, e, c, 1 - y, right(2)], RX1.at[e, 1, 1], 5, to_x(3))

    def sums_y1(e):
        return sum_copy(1, e, PART.at[1, e, c, 1 - y, x], RY1.at[e], 4, to_y)

    def add(a, b):
        return (a.astype(F32) + b.astype(F32)).astype(BF16)

    def add_core(a, e):
        sums_core(a, e).wait_recv()
        PART[a, e, c] = add(PART[a, e, c], SIB[a, e])
        if a == 0:
            sums_y0(e).start()
        else:
            sums_on_right(e).start()
            sums_on_left(e).start()

    def add_second(a, e):
        if a == 0:
            sums_y0(e).wait_recv()
            PART[0, e, c, y] = add(PART[0, e, c, y], RY0[e])
            for k in range(1, NX):
                sums_x0(e, k).start()
        else:
            sums_on_right(e).wait_recv()
            PART[1, e, c, y, right(1)] = add(PART[1, e, c, y, right(1)], RX1[e, 1, 0])
            sums_on_left(e).wait_recv()
            PART[1, e, c, 1 - y, left(1)] = add(PART[1, e, c, 1 - y, left(1)], RX1[e, 1, 1])
            for k in (1, 3):
                sums_x1(e, k).start()

    def add_third(a, e):
        if a == 0:
            total = PART[0, e, c, y, x].astype(F32)
            for k in range(1, NX):
                sums_x0(e, k).wait_recv()
                total = total + RX0[e, k - 1].astype(F32)
            FIN[0, e] = total.astype(BF16)
        else:
            total = PART[1, e, c, :, x].astype(F32)
            for k in (1, 3):
                sums_x1(e, k).wait_recv()
                total = total + RX1[e, k - 1].astype(F32)
            PART[1, e, c, :, x] = total.astype(BF16)
            sums_y1(e).start()

    def add_fourth(a, e):
        sums_y1(e).wait_recv()
        FIN[1, e] = add(PART[1, e, c, y, x], RY1[e])

    for load in loads[3:]:
        load.wait()
    def back(part, k):
        return remote(
            BACK.at[part, ex_to(k)], BACK_IN.at[part, ex], back_s.at[part, k], back_r.at[part, k], (dp, ex_to(k))
        )

    def send_back(a, part):
        flat = halves(FIN[:, 2 * part:2 * part + 2].reshape(SLOT_ROWS // PARTS, D))
        rows = [dot(BY_MESSAGE[j], flat[j]) for j in range(2)]
        BACK[part] = (rows[0] + rows[1]).astype(BF16).reshape(GROUPS, ROWS, D // 2)
        for k in FAR_FIRST:
            back(part, k).start()
        BACK_IN[part, ex] = BACK[part, ex]

    steps = {
        "A": arrive, "G": lambda a, e: gather_first(a, e, start), "S": second, "O": second_on, "T": third,
        "X": expert, "C": add_core, "D": add_second, "E": add_third, "F": add_fourth, "B": send_back,
    }
    for line in ORDER:
        for word in line.split():
            steps[word[0]](int(word[1]), int(word[2]))

    def grads(e, carry):
        weight_grads(e)
        return carry

    lax.fori_loop(0, LOCAL, grads, 0)
    for k in range(1, GROUPS):
        back(0, k).wait_recv()
    first = [dot(BY_SLOT[0, j], BACK_IN[0].reshape(SLOT_ROWS, D // 2)) for j in range(2)]
    for k in range(1, GROUPS):
        back(1, k).wait_recv()
    for j in range(2):
        rows = first[j] + dot(BY_SLOT[1, j], BACK_IN[1].reshape(SLOT_ROWS, D // 2))
        SUMS[:, :, :, j * (D // 2):(j + 1) * (D // 2)] = rows.astype(BF16).reshape(2, IMGS, SLOTS, D // 2)

    param = jnp.zeros((SLOTS, D), F32)
    logit_grads = []
    for i in range(IMGS):
        dispatch, combine = DI[i], CO[i]
        combine_grad = dot(SUMS[0, i], G[i], 1, 1)
        dispatch_grad = dot(SUMS[1, i], T[i], 1, 1)
        combine_term = combine * (combine_grad - jnp.sum(combine * combine_grad, axis=0, keepdims=True))
        dispatch_term = dispatch * (dispatch_grad - jnp.sum(dispatch * dispatch_grad, axis=1, keepdims=True))
        logit_grad = (combine_term + dispatch_term).astype(BF16)
        logit_grads.append(logit_grad)
        param = param + dot(logit_grad, T[i])

    for j in range(GROUPS * SHARE):
        tile = slice(8 * (j % SHARE), 8 * (j % SHARE) + 8)
        PP[j // SHARE, tile] = param[8 * (j // 10):8 * (j // 10) + 8, 128 * (j % 10):128 * (j % 10) + 128]

    def ar_scatter(k):
        other, device = to_member(k)
        return remote(PP.at[other], AR1.at[k - 1], ar_s.at[k], ar_r.at[k], device)

    def ar_plane(k):
        return remote(AR2.at[plane], AR2.at[plane], mid_s.at[k], mid_r.at[k], to_plane(k))

    def ar_gather(k):
        return remote(GP.at[member], GP.at[member], last_s.at[k], last_r.at[k], to_member(k)[1])

    for k in FAR_FIRST:
        ar_scatter(k).start()

    for i in range(IMGS):
        both = jnp.concatenate([DI[i].astype(BF16), logit_grads[i]], axis=0)
        rows = jnp.concatenate([SUMS[1, i], SP[...]], axis=0)
        grad_tokens[i] = dot(both.T, rows).astype(BF16)

    total = PP[member]
    for k in range(1, GROUPS):
        ar_scatter(k).wait_recv()
        total = total + AR1[k - 1]
    AR2[plane, :8 * SHARE] = total.astype(BF16)
    AR2[plane, 8 * SHARE:] = jnp.zeros((8, 128), BF16)
    for k in PLANE_FAR_FIRST:
        ar_plane(k).start()
    for k in range(1, NX * NY * NH):
        ar_plane(k).wait_recv()
    total = AR2[0, :8 * SHARE].astype(F32)
    for k in range(1, NX * NY * NH):
        total = total + AR2[k, :8 * SHARE].astype(F32)
    GP[member] = total
    for k in FAR_FIRST:
        ar_gather(k).start()

    def drain(e, carry):
        for a in range(2):
            gather_first(a, e, wait_send)
            gather_third(a, e).wait_send()
            sums_core(a, e).wait_send()
        gather_on_right(e, wait_send)
        gather_on_left(e, wait_send)
        for k in range(1, NX):
            gather_second_y(e, wait_send, k)
            sums_x0(e, k).wait_send()
        for k in (1, 3):
            gather_second_x(e, wait_send, k)
            sums_x1(e, k).wait_send()
        sums_on_right(e).wait_send()
        sums_on_left(e).wait_send()
        sums_y0(e).wait_send()
        sums_y1(e).wait_send()
        return carry

    lax.fori_loop(0, LOCAL, drain, 0)
    for k in range(1, GROUPS):
        for part in range(PARTS):
            a2a(part, k).wait_send()
            back(part, k).wait_send()
        ar_scatter(k).wait_send()
    for k in range(1, NX * NY * NH):
        ar_plane(k).wait_send()
    for k in range(1, GROUPS):
        ar_gather(k).wait_recv()
    for k in range(1, GROUPS):
        ar_gather(k).wait_send()
    for j in range(GROUPS * SHARE):
        tile = slice(8 * (j % SHARE), 8 * (j % SHARE) + 8)
        grad_param[8 * (j // 10):8 * (j // 10) + 8, 128 * (j % 10):128 * (j % 10) + 128] = GP[j // SHARE, tile]


def write_out(*refs):
    pairs = [(refs[1], refs[5])]
    for i in (0, 2, 3):
        pairs += [(refs[i].at[j], refs[4 + i].at[j]) for j in range(refs[i].shape[0])]
    copies = [pltpu.make_async_copy(*pair, refs[8].at[i]) for i, pair in enumerate(pairs)]
    for copy in copies:
        copy.start()
    for copy in copies:
        copy.wait()


def on_device(tokens, slot_param, inner_weight, outer_weight, output_grad):
    vmem = pl.BlockSpec(memory_space=pltpu.VMEM)
    chunk = (8 * SHARE, 128)
    dma = pltpu.SemaphoreType.DMA
    results = pl.pallas_call(
        kernel,
        out_shape=(
            pltpu.VMEM(tokens.shape, BF16),
            pltpu.VMEM(slot_param.shape, F32),
            pltpu.VMEM(inner_weight.shape, BF16),
            pltpu.VMEM(outer_weight.shape, BF16),
        ),
        in_specs=[pl.BlockSpec(memory_space=pltpu.HBM)] * 5,
        out_specs=(vmem,) * 4,
        scratch_shapes=[
            pltpu.VMEM((IMGS, PATCHES, D), BF16),
            pltpu.VMEM((IMGS, PATCHES, D), BF16),
            pltpu.VMEM((SLOTS, D), BF16),
            pltpu.VMEM((LOCAL, HIDDEN, D), BF16),
            pltpu.VMEM((LOCAL, HIDDEN, D), BF16),
            pltpu.VMEM((IMGS, SLOTS, PATCHES), F32),
            pltpu.VMEM((IMGS, SLOTS, PATCHES), F32),
            pltpu.VMEM((2 * IMGS, SLOTS, D), BF16),
            pltpu.VMEM((PARTS, GROUPS, ROWS, D // 2), BF16),
            pltpu.VMEM((PARTS, GROUPS, ROWS, D // 2), BF16),
            pltpu.VMEM((PARTS, GROUPS, ROWS, D // 2), BF16),
            pltpu.VMEM((PARTS, GROUPS, ROWS, D // 2), BF16),
            pltpu.VMEM((2, LOCAL, ROWS, D), BF16),
            pltpu.VMEM((2, IMGS, SLOTS, D), BF16),
            pltpu.VMEM((2, SLOT_ROWS // PARTS, SLOT_ROWS), BF16),
            pltpu.VMEM((2, SLOT_ROWS, SLOT_ROWS // PARTS), BF16),
            pltpu.VMEM((PARTS, 2, SLOT_ROWS, SLOT_ROWS), BF16),
            pltpu.VMEM((2, LOCAL, NC, NY, NX, ROWS, D), BF16),
            pltpu.VMEM((LOCAL, HIDDEN, BLOCKS * ROWS), BF16),
            pltpu.VMEM((LOCAL, HIDDEN, BLOCKS * ROWS), BF16),
            pltpu.VMEM((LOCAL, HIDDEN, BLOCKS * ROWS), F32),
            pltpu.VMEM((2, LOCAL, NC, NY, NX, ROWS, D), BF16),
            pltpu.VMEM((2, LOCAL, NY, NX, ROWS, D), BF16),
            pltpu.VMEM((LOCAL, NX, ROWS, D), BF16),
            pltpu.VMEM((LOCAL, NX - 1, ROWS, D), BF16),
            pltpu.VMEM((LOCAL, ROWS, D), BF16),
            pltpu.VMEM((LOCAL, NX - 1, NY, ROWS, D), BF16),
            pltpu.VMEM((GROUPS,) + chunk, F32),
            pltpu.VMEM((GROUPS - 1,) + chunk, F32),
            pltpu.VMEM((NX * NY * NH, 8 * SHARE + 8, 128), BF16),
            pltpu.VMEM((GROUPS,) + chunk, F32),
            dma((5,)), dma((PARTS, GROUPS)), dma((PARTS, GROUPS)), dma((PARTS, GROUPS)), dma((PARTS, GROUPS)),
            dma((2, LOCAL, 8)), dma((2, LOCAL, 8)), dma((2, LOCAL, 6)), dma((2, LOCAL, 6)),
            dma((GROUPS,)), dma((GROUPS,)), dma((NX * NY * NH,)), dma((NX * NY * NH,)),
            dma((GROUPS,)), dma((GROUPS,)),
        ],
        compiler_params=pltpu.CompilerParams(
            collective_id=0, has_side_effects=True, vmem_limit_bytes=54 * 2**20
        ),
    )(tokens, slot_param, inner_weight, outer_weight, output_grad)
    return pl.pallas_call(
        write_out,
        out_shape=tuple(jax.ShapeDtypeStruct(result.shape, result.dtype) for result in results),
        in_specs=[vmem] * 4,
        out_specs=(pl.BlockSpec(memory_space=pltpu.HBM),) * 4,
        scratch_shapes=[dma((1 + IMGS + 2 * LOCAL,))],
        compiler_params=pltpu.CompilerParams(vmem_limit_bytes=2**20),
    )(*[pltpu.with_memory_space_constraint(result, pltpu.VMEM) for result in results])


def solution(mesh):
    in_specs = (
        P(("dp", "expert"), None, None),
        P(),
        P("expert", "dp", None),
        P("expert", "dp", None),
        P(("dp", "expert"), None, None),
    )
    out_specs = (
        P(("dp", "expert"), None, None),
        P(),
        P("expert", "dp", None),
        P("expert", "dp", None),
    )
    return jax.shard_map(
        on_device, mesh=mesh, in_specs=in_specs, out_specs=out_specs, check_vma=False
    )
```

```python
import functools

import jax
import jax.numpy as jnp
from jax import lax
from jax.experimental import pallas as pl
from jax.experimental.pallas import tpu as pltpu
from jax.sharding import PartitionSpec as P

MESH = pl.DeviceIdType.MESH
F32 = jnp.float32
BF16 = jnp.bfloat16
NX, NY, NC = 4, 2, 2
NH, NZ = 2, 4
GROUPS = NH * NZ
FAR_FIRST = (6, 5, 7, 2, 4, 1, 3)
PLANE_FAR_FIRST = (11, 9, 10, 7, 15, 8, 5, 13, 6, 14, 3, 1, 4, 12, 2)
LOCAL = 4
IMGS = 2
SLOTS = GROUPS * LOCAL
ROWS = 16
BLOCKS = NC * NY * NX
D = 1280
PATCHES = 256
HIDDEN = 320
TILE = 256
STEPS = D // TILE
PARTS = 2
SLOT_ROWS = 2 * IMGS * SLOTS
SHARE = SLOTS * D // (8 * 128 * GROUPS)

ORDER = (
    "A00 G01 G00 G10",
    "G11 A01 G12 G02",
    "S01 S10 G13 S00",
    "S11 G03 T01 O10",
    "S02 S12 X01 O11",
    "T00 S13 C01 T10",
    "X00 O12 T11 S03",
    "X10 T02 O13 C00",
    "X11 C10 T12 X02",
    "C11 D01 X12 C02",
    "T03 D10 T13 C12",
    "X03 D11 X13 C13",
    "D00 C03 D12 D13",
    "E11 D02 E10 E12",
    "E01 D03 F10 E00",
    "E13 F12 F11 B00",
    "E02 F13 E03 B01",
)


def dot(a, b, ca=1, cb=0):
    return lax.dot_general(a, b, (((ca,), (cb,)), ((), ())), preferred_element_type=F32)


def place(rows, columns, source_of, part, half, transposed=False):
    shape = (columns, rows) if transposed else (rows, columns)
    row = lax.broadcasted_iota(jnp.int32, shape, 1 if transposed else 0)
    column = lax.broadcasted_iota(jnp.int32, shape, 0 if transposed else 1)
    source, in_half = source_of(row, part, half)
    return jnp.where(jnp.logical_and(column == source, in_half), 1.0, 0.0).astype(BF16)


def slots_of_message(r, part, half):
    group, array, expert, image = r // 16, (r // 4) % 2, (r // 2) % 2, r % 2
    return array * 64 + image * 32 + group * 4 + 2 * part + expert, (r // 8) % 2 == half


def message_of_blocks(r, part, half):
    array, expert, group, image = r // 32, (r // 16) % 2, (r // 2) % 8, r % 2
    return group * 16 + half * 8 + array * 4 + expert * 2 + image, r >= 0


def halves(array):
    return array[:, : D // 2], array[:, D // 2 :]


def kernel(
    tokens, slot_param, inner, outer, cotangent,
    grad_tokens, grad_param, grad_inner, grad_outer,
    T, G, SP, WI, WO, DI, CO, X, MSG, MSG_IN, BACK, BACK_IN, FIN, SUMS, BY_BLOCK, BY_MESSAGE, BY_SLOT,
    R, ACT, SCA, SLOPE, PART, SIB, RY0, RX0, RY1, RX1,
    PP, AR1, AR2, GP,
    in_sem, a2a_s, a2a_r, back_s, back_r, ag_s, ag_r, rs_s, rs_r, ar_s, ar_r, mid_s, mid_r, last_s, last_r,
):
    dp, ex = lax.axis_index("dp"), lax.axis_index("expert")
    x, y, c = dp // 4, (dp // 2) % 2, dp % 2
    h, z = ex // NZ, ex % NZ

    def at_dp(px, py, pc):
        return (px * 4 + py * 2 + pc, ex)

    def right(k):
        return (x + k) % NX

    def left(k):
        return (x + NX - k) % NX

    def to_x(k):
        return at_dp(right(k), y, c)

    to_y = at_dp(x, 1 - y, c)
    to_core = at_dp(x, y, 1 - c)

    def ex_to(k):
        return (h + k // NZ) % NH * NZ + (z + k) % NZ

    def remote(src, dst, send, recv, device):
        return pltpu.make_async_remote_copy(
            src_ref=src, dst_ref=dst, send_sem=send, recv_sem=recv, device_id=device, device_id_type=MESH
        )

    member = c * NZ + z
    plane = (x * NY + y) * NH + h

    def to_member(k):
        core, depth = (c + k // NZ) % NC, (z + k) % NZ
        return core * NZ + depth, ((x * NY + y) * NC + core, h * NZ + depth)

    def to_plane(k):
        device = at_dp((x + k // 4) % NX, (y + k // 2) % NY, c)[0]
        return device, (h + k) % NH * NZ + z

    barrier = pltpu.get_barrier_semaphore()
    partners = [
        (at_dp(right(dx), (y + dy) % NY, c)[0], (h + dh) % NH * NZ + z)
        for dx in (2, 1, 3, 0) for dh in (1, 0) for dy in (1, 0) if dx or dy
    ]
    partners += [(dp, ex_to(k)) for k in range(GROUPS - 1, 0, -1)]
    partners += [(at_dp(x, y, 1 - c)[0], h * NZ + (z + k) % NZ) for k in range(1, NZ)] + [to_core]
    for partner in partners:
        pl.semaphore_signal(barrier, inc=1, device_id=partner, device_id_type=MESH)

    loads = [
        pltpu.make_async_copy(slot_param, SP, in_sem.at[0]),
        pltpu.make_async_copy(tokens, T, in_sem.at[1]),
        pltpu.make_async_copy(cotangent, G, in_sem.at[2]),
        pltpu.make_async_copy(inner, WI, in_sem.at[3]),
        pltpu.make_async_copy(outer, WO, in_sem.at[4]),
    ]
    for load in loads:
        load.start()
    for load in loads[:3]:
        load.wait()

    for i in range(IMGS):
        logits = dot(SP[...], T[i], 1, 1)
        ed = jnp.exp(logits - jnp.max(logits, axis=1, keepdims=True))
        dispatch = ed / jnp.sum(ed, axis=1, keepdims=True)
        ec = jnp.exp(logits - jnp.max(logits, axis=0, keepdims=True))
        combine = ec / jnp.sum(ec, axis=0, keepdims=True)
        DI[i] = dispatch
        CO[i] = combine
        X[i] = dot(dispatch.astype(BF16), T[i]).astype(BF16)
        X[IMGS + i] = dot(combine.astype(BF16), G[i]).astype(BF16)
    for j in range(2):
        BY_BLOCK[j] = place(SLOT_ROWS // PARTS, SLOT_ROWS, message_of_blocks, 0, j)
        BY_MESSAGE[j] = place(SLOT_ROWS // PARTS, SLOT_ROWS, message_of_blocks, 0, j, True)
        for part in range(PARTS):
            BY_SLOT[part, j] = place(SLOT_ROWS, SLOT_ROWS, slots_of_message, part, j, True)
    flat = halves(X[...].reshape(SLOT_ROWS, D))
    for part in range(PARTS):
        rows = [dot(place(SLOT_ROWS, SLOT_ROWS, slots_of_message, part, j), flat[j]) for j in range(2)]
        MSG[part] = (rows[0] + rows[1]).astype(BF16).reshape(GROUPS, ROWS, D // 2)

    pl.semaphore_wait(barrier, len(partners))

    def a2a(part, k):
        return remote(
            MSG.at[part, ex_to(k)], MSG_IN.at[part, ex], a2a_s.at[part, k], a2a_r.at[part, k], (dp, ex_to(k))
        )

    for part in range(PARTS):
        for k in FAR_FIRST:
            a2a(part, k).start()
    for part in range(PARTS):
        MSG_IN[part, ex] = MSG[part, ex]

    def arrive(a, part):
        for k in range(1, GROUPS):
            a2a(part, k).wait_recv()
        flat = MSG_IN[part].reshape(SLOT_ROWS, D // 2)
        for j in range(2):
            rows = dot(BY_BLOCK[j], flat).astype(BF16)
            rows = rows.reshape(2, LOCAL // PARTS, ROWS, D // 2)
            for a in range(2):
                for e in range(LOCAL // PARTS):
                    R[a, 2 * part + e, c, y, x, :, j * (D // 2):(j + 1) * (D // 2)] = rows[a, e]

    def block_copy(a, e, py, px, sem, device):
        ref = R.at[a, e, c, py, px]
        return remote(ref, ref, ag_s.at[a, e, sem], ag_r.at[a, e, sem], device)

    def gather_first(a, e, act):
        if a == 1:
            act(block_copy(1, e, y, x, 3, to_y))
        for k in range(1, NX) if a == 0 else (1, 3):
            act(block_copy(a, e, y, x, k - 1, to_x(k)))
        if a == 0:
            act(block_copy(0, e, y, x, 3, to_y))

    def gather_second_x(e, act, k):
        act(block_copy(1, e, 1 - y, x, 3 + k, to_x(k)))

    def gather_second_y(e, act, k):
        act(block_copy(0, e, y, left(k), 3 + k, to_y))

    def gather_on_right(e, act):
        act(block_copy(1, e, y, left(1), 1, to_x(1)))

    def gather_on_left(e, act):
        act(block_copy(1, e, 1 - y, right(1), 5, to_x(3)))

    def gather_third(a, e, j):
        ref = R.at[a, e, c, (y + j) % NY]
        return remote(ref, ref, ag_s.at[a, e, 7 + j], ag_r.at[a, e, 7 + j], to_core)

    def start(copy):
        copy.start()

    def wait_send(copy):
        copy.wait_send()

    def wait_recv(a, e, sem):
        block_copy(a, e, y, x, sem, to_y).wait_recv()

    def second(a, e):
        if a == 0:
            for k in (1, 3, 2):
                wait_recv(0, e, k - 1)
                gather_second_y(e, start, k)
            gather_third(0, e, 0).start()
        else:
            wait_recv(1, e, 3)
            for k in (1, 3):
                gather_second_x(e, start, k)
            wait_recv(1, e, 0)
            gather_on_right(e, start)

    def second_on(a, e):
        wait_recv(1, e, 6)
        gather_on_left(e, start)

    def third(a, e):
        for sem in (3, 4, 5, 6) if a == 0 else (2, 1, 4, 5):
            wait_recv(a, e, sem)
        if a == 1:
            gather_third(1, e, 0).start()
        gather_third(a, e, 1).start()

    def expert(a, e):
        for j in range(NY):
            gather_third(a, e, j).wait_recv()
        rows = R[a, e].reshape(BLOCKS * ROWS, D)
        if a == 0:
            hidden = dot(WI[e], rows, 1, 1)
            phi = 0.5 * (1.0 + lax.erf(hidden * 0.7071067811865476))
            SLOPE[e] = phi + hidden * jnp.exp(-0.5 * hidden * hidden) * 0.3989422804014327
            act, kept, weight = (hidden * phi).astype(BF16), ACT, WO
        else:
            act, kept, weight = (dot(WO[e], rows, 1, 1) * SLOPE[e]).astype(BF16), SCA, WI
        kept[e] = act
        act_t = act.T
        for n in range(STEPS):
            cols = slice(n * TILE, (n + 1) * TILE)
            PART[a, e, :, :, :, :, cols] = (
                dot(act_t, weight[e, :, cols]).astype(BF16).reshape(NC, NY, NX, ROWS, TILE)
            )
        sums_core(a, e).start()

    def weight_grads(e):
        for n in range(STEPS):
            cols = slice(n * TILE, (n + 1) * TILE)
            rows_in = R[0, e, :, :, :, :, cols].reshape(BLOCKS * ROWS, TILE)
            rows_grad = R[1, e, :, :, :, :, cols].reshape(BLOCKS * ROWS, TILE)
            grad_outer[e, :, cols] = dot(ACT[e], rows_grad).astype(BF16)
            grad_inner[e, :, cols] = dot(SCA[e], rows_in).astype(BF16)

    def sum_copy(a, e, src, dst, sem, device):
        return remote(src, dst, rs_s.at[a, e, sem], rs_r.at[a, e, sem], device)

    def sums_core(a, e):
        return sum_copy(a, e, PART.at[a, e, 1 - c], SIB.at[a, e], 0, to_core)

    def sums_y0(e):
        return sum_copy(0, e, PART.at[0, e, c, 1 - y], RY0.at[e], 4, to_y)

    def sums_x0(e, k):
        return sum_copy(0, e, PART.at[0, e, c, y, right(k)], RX0.at[e, k - 1], k, to_x(k))

    def sums_x1(e, k):
        return sum_copy(1, e, PART.at[1, e, c, :, right(k)], RX1.at[e, k - 1], k, to_x(k))

    def sums_on_right(e):
        return sum_copy(1, e, PART.at[1, e, c, y, right(2)], RX1.at[e, 1, 0], 2, to_x(1))

    def sums_on_left(e):
        return sum_copy(1, e, PART.at[1, e, c, 1 - y, right(2)], RX1.at[e, 1, 1], 5, to_x(3))

    def sums_y1(e):
        return sum_copy(1, e, PART.at[1, e, c, 1 - y, x], RY1.at[e], 4, to_y)

    def add(a, b):
        return (a.astype(F32) + b.astype(F32)).astype(BF16)

    def add_core(a, e):
        sums_core(a, e).wait_recv()
        PART[a, e, c] = add(PART[a, e, c], SIB[a, e])
        if a == 0:
            sums_y0(e).start()
        else:
            sums_on_right(e).start()
            sums_on_left(e).start()

    def add_second(a, e):
        if a == 0:
            sums_y0(e).wait_recv()
            PART[0, e, c, y] = add(PART[0, e, c, y], RY0[e])
            for k in range(1, NX):
                sums_x0(e, k).start()
        else:
            sums_on_right(e).wait_recv()
            PART[1, e, c, y, right(1)] = add(PART[1, e, c, y, right(1)], RX1[e, 1, 0])
            sums_on_left(e).wait_recv()
            PART[1, e, c, 1 - y, left(1)] = add(PART[1, e, c, 1 - y, left(1)], RX1[e, 1, 1])
            for k in (1, 3):
                sums_x1(e, k).start()

    def add_third(a, e):
        if a == 0:
            total = PART[0, e, c, y, x].astype(F32)
            for k in range(1, NX):
                sums_x0(e, k).wait_recv()
                total = total + RX0[e, k - 1].astype(F32)
            FIN[0, e] = total.astype(BF16)
        else:
            total = PART[1, e, c, :, x].astype(F32)
            for k in (1, 3):
                sums_x1(e, k).wait_recv()
                total = total + RX1[e, k - 1].astype(F32)
            PART[1, e, c, :, x] = total.astype(BF16)
            sums_y1(e).start()

    def add_fourth(a, e):
        sums_y1(e).wait_recv()
        FIN[1, e] = add(PART[1, e, c, y, x], RY1[e])

    for load in loads[3:]:
        load.wait()
    def back(part, k):
        return remote(
            BACK.at[part, ex_to(k)], BACK_IN.at[part, ex], back_s.at[part, k], back_r.at[part, k], (dp, ex_to(k))
        )

    def send_back(a, part):
        flat = halves(FIN[:, 2 * part:2 * part + 2].reshape(SLOT_ROWS // PARTS, D))
        rows = [dot(BY_MESSAGE[j], flat[j]) for j in range(2)]
        BACK[part] = (rows[0] + rows[1]).astype(BF16).reshape(GROUPS, ROWS, D // 2)
        for k in FAR_FIRST:
            back(part, k).start()
        BACK_IN[part, ex] = BACK[part, ex]

    steps = {
        "A": arrive, "G": lambda a, e: gather_first(a, e, start), "S": second, "O": second_on, "T": third,
        "X": expert, "C": add_core, "D": add_second, "E": add_third, "F": add_fourth, "B": send_back,
    }
    for line in ORDER:
        for word in line.split():
            steps[word[0]](int(word[1]), int(word[2]))

    def grads(e, carry):
        weight_grads(e)
        return carry

    lax.fori_loop(0, LOCAL, grads, 0)
    for k in range(1, GROUPS):
        back(0, k).wait_recv()
    first = [dot(BY_SLOT[0, j], BACK_IN[0].reshape(SLOT_ROWS, D // 2)) for j in range(2)]
    for k in range(1, GROUPS):
        back(1, k).wait_recv()
    for j in range(2):
        rows = first[j] + dot(BY_SLOT[1, j], BACK_IN[1].reshape(SLOT_ROWS, D // 2))
        SUMS[:, :, :, j * (D // 2):(j + 1) * (D // 2)] = rows.astype(BF16).reshape(2, IMGS, SLOTS, D // 2)

    param = jnp.zeros((SLOTS, D), F32)
    logit_grads = []
    for i in range(IMGS):
        dispatch, combine = DI[i], CO[i]
        combine_grad = dot(SUMS[0, i], G[i], 1, 1)
        dispatch_grad = dot(SUMS[1, i], T[i], 1, 1)
        combine_term = combine * (combine_grad - jnp.sum(combine * combine_grad, axis=0, keepdims=True))
        dispatch_term = dispatch * (dispatch_grad - jnp.sum(dispatch * dispatch_grad, axis=1, keepdims=True))
        logit_grad = (combine_term + dispatch_term).astype(BF16)
        logit_grads.append(logit_grad)
        param = param + dot(logit_grad, T[i])

    for j in range(GROUPS * SHARE):
        tile = slice(8 * (j % SHARE), 8 * (j % SHARE) + 8)
        PP[j // SHARE, tile] = param[8 * (j // 10):8 * (j // 10) + 8, 128 * (j % 10):128 * (j % 10) + 128]

    def ar_scatter(k):
        other, device = to_member(k)
        return remote(PP.at[other], AR1.at[k - 1], ar_s.at[k], ar_r.at[k], device)

    def ar_plane(k):
        return remote(AR2.at[plane], AR2.at[plane], mid_s.at[k], mid_r.at[k], to_plane(k))

    def ar_gather(k):
        return remote(GP.at[member], GP.at[member], last_s.at[k], last_r.at[k], to_member(k)[1])

    for k in FAR_FIRST:
        ar_scatter(k).start()

    for i in range(IMGS):
        both = jnp.concatenate([DI[i].astype(BF16), logit_grads[i]], axis=0)
        rows = jnp.concatenate([SUMS[1, i], SP[...]], axis=0)
        grad_tokens[i] = dot(both.T, rows).astype(BF16)

    total = PP[member]
    for k in range(1, GROUPS):
        ar_scatter(k).wait_recv()
        total = total + AR1[k - 1]
    AR2[plane, :8 * SHARE] = total.astype(BF16)
    AR2[plane, 8 * SHARE:] = jnp.zeros((8, 128), BF16)
    for k in PLANE_FAR_FIRST:
        ar_plane(k).start()
    for k in range(1, NX * NY * NH):
        ar_plane(k).wait_recv()
    total = AR2[0, :8 * SHARE].astype(F32)
    for k in range(1, NX * NY * NH):
        total = total + AR2[k, :8 * SHARE].astype(F32)
    GP[member] = total
    for k in FAR_FIRST:
        ar_gather(k).start()

    def drain(e, carry):
        for a in range(2):
            gather_first(a, e, wait_send)
            for j in range(NY):
                gather_third(a, e, j).wait_send()
            sums_core(a, e).wait_send()
        gather_on_right(e, wait_send)
        gather_on_left(e, wait_send)
        for k in range(1, NX):
            gather_second_y(e, wait_send, k)
            sums_x0(e, k).wait_send()
        for k in (1, 3):
            gather_second_x(e, wait_send, k)
            sums_x1(e, k).wait_send()
        sums_on_right(e).wait_send()
        sums_on_left(e).wait_send()
        sums_y0(e).wait_send()
        sums_y1(e).wait_send()
        return carry

    lax.fori_loop(0, LOCAL, drain, 0)
    for k in range(1, GROUPS):
        for part in range(PARTS):
            a2a(part, k).wait_send()
            back(part, k).wait_send()
        ar_scatter(k).wait_send()
    for k in range(1, NX * NY * NH):
        ar_plane(k).wait_send()
    for k in range(1, GROUPS):
        ar_gather(k).wait_recv()
    for k in range(1, GROUPS):
        ar_gather(k).wait_send()
    for j in range(GROUPS * SHARE):
        tile = slice(8 * (j % SHARE), 8 * (j % SHARE) + 8)
        grad_param[8 * (j // 10):8 * (j // 10) + 8, 128 * (j % 10):128 * (j % 10) + 128] = GP[j // SHARE, tile]


def write_out(*refs):
    pairs = [(refs[1], refs[5])]
    for i in (0, 2, 3):
        pairs += [(refs[i].at[j], refs[4 + i].at[j]) for j in range(refs[i].shape[0])]
    copies = [pltpu.make_async_copy(*pair, refs[8].at[i]) for i, pair in enumerate(pairs)]
    for copy in copies:
        copy.start()
    for copy in copies:
        copy.wait()


def on_device(tokens, slot_param, inner_weight, outer_weight, output_grad):
    vmem = pl.BlockSpec(memory_space=pltpu.VMEM)
    chunk = (8 * SHARE, 128)
    dma = pltpu.SemaphoreType.DMA
    results = pl.pallas_call(
        kernel,
        out_shape=(
            pltpu.VMEM(tokens.shape, BF16),
            pltpu.VMEM(slot_param.shape, F32),
            pltpu.VMEM(inner_weight.shape, BF16),
            pltpu.VMEM(outer_weight.shape, BF16),
        ),
        in_specs=[pl.BlockSpec(memory_space=pltpu.HBM)] * 5,
        out_specs=(vmem,) * 4,
        scratch_shapes=[
            pltpu.VMEM((IMGS, PATCHES, D), BF16),
            pltpu.VMEM((IMGS, PATCHES, D), BF16),
            pltpu.VMEM((SLOTS, D), BF16),
            pltpu.VMEM((LOCAL, HIDDEN, D), BF16),
            pltpu.VMEM((LOCAL, HIDDEN, D), BF16),
            pltpu.VMEM((IMGS, SLOTS, PATCHES), F32),
            pltpu.VMEM((IMGS, SLOTS, PATCHES), F32),
            pltpu.VMEM((2 * IMGS, SLOTS, D), BF16),
            pltpu.VMEM((PARTS, GROUPS, ROWS, D // 2), BF16),
            pltpu.VMEM((PARTS, GROUPS, ROWS, D // 2), BF16),
            pltpu.VMEM((PARTS, GROUPS, ROWS, D // 2), BF16),
            pltpu.VMEM((PARTS, GROUPS, ROWS, D // 2), BF16),
            pltpu.VMEM((2, LOCAL, ROWS, D), BF16),
            pltpu.VMEM((2, IMGS, SLOTS, D), BF16),
            pltpu.VMEM((2, SLOT_ROWS // PARTS, SLOT_ROWS), BF16),
            pltpu.VMEM((2, SLOT_ROWS, SLOT_ROWS // PARTS), BF16),
            pltpu.VMEM((PARTS, 2, SLOT_ROWS, SLOT_ROWS), BF16),
            pltpu.VMEM((2, LOCAL, NC, NY, NX, ROWS, D), BF16),
            pltpu.VMEM((LOCAL, HIDDEN, BLOCKS * ROWS), BF16),
            pltpu.VMEM((LOCAL, HIDDEN, BLOCKS * ROWS), BF16),
            pltpu.VMEM((LOCAL, HIDDEN, BLOCKS * ROWS), F32),
            pltpu.VMEM((2, LOCAL, NC, NY, NX, ROWS, D), BF16),
            pltpu.VMEM((2, LOCAL, NY, NX, ROWS, D), BF16),
            pltpu.VMEM((LOCAL, NX, ROWS, D), BF16),
            pltpu.VMEM((LOCAL, NX - 1, ROWS, D), BF16),
            pltpu.VMEM((LOCAL, ROWS, D), BF16),
            pltpu.VMEM((LOCAL, NX - 1, NY, ROWS, D), BF16),
            pltpu.VMEM((GROUPS,) + chunk, F32),
            pltpu.VMEM((GROUPS - 1,) + chunk, F32),
            pltpu.VMEM((NX * NY * NH, 8 * SHARE + 8, 128), BF16),
            pltpu.VMEM((GROUPS,) + chunk, F32),
            dma((5,)), dma((PARTS, GROUPS)), dma((PARTS, GROUPS)), dma((PARTS, GROUPS)), dma((PARTS, GROUPS)),
            dma((2, LOCAL, 9)), dma((2, LOCAL, 9)), dma((2, LOCAL, 6)), dma((2, LOCAL, 6)),
            dma((GROUPS,)), dma((GROUPS,)), dma((NX * NY * NH,)), dma((NX * NY * NH,)),
            dma((GROUPS,)), dma((GROUPS,)),
        ],
        compiler_params=pltpu.CompilerParams(
            collective_id=0, has_side_effects=True, vmem_limit_bytes=54 * 2**20
        ),
    )(tokens, slot_param, inner_weight, outer_weight, output_grad)
    return pl.pallas_call(
        write_out,
        out_shape=tuple(jax.ShapeDtypeStruct(result.shape, result.dtype) for result in results),
        in_specs=[vmem] * 4,
        out_specs=(pl.BlockSpec(memory_space=pltpu.HBM),) * 4,
        scratch_shapes=[dma((1 + IMGS + 2 * LOCAL,))],
        compiler_params=pltpu.CompilerParams(vmem_limit_bytes=2**20),
    )(*[pltpu.with_memory_space_constraint(result, pltpu.VMEM) for result in results])


def solution(mesh):
    in_specs = (
        P(("dp", "expert"), None, None),
        P(),
        P("expert", "dp", None),
        P("expert", "dp", None),
        P(("dp", "expert"), None, None),
    )
    out_specs = (
        P(("dp", "expert"), None, None),
        P(),
        P("expert", "dp", None),
        P("expert", "dp", None),
    )
    return jax.shard_map(
        on_device, mesh=mesh, in_specs=in_specs, out_specs=out_specs, check_vma=False
    )
```
